256 devices in a mesh: tm: 128 (over x, y, z), row: 2 (over core).
Axes of the slice: x: 4, y: 4, z: 8, core: 2. Of those that a mesh axis runs over, the one named last changes fastest.
Arguments:
- decay_fwd: float32 [256, 256], P('tm'), may hold values from 0.4 to 1
- decay_bwd: float32 [256, 256], P('tm'), may hold values from 0.4 to 1
- angle: float32 [256], P('tm'), may hold values from 0.2 to 0.5
- gain: float32 [256, 256], P('tm'), may hold values from 0.02 to 0.1
- obs_values: float32 [256, 64, 128], P('tm'), may hold values from -6 to 6
- obs_sites: int32 [256, 64], P('tm'), may hold values from 0 to 127
- obs_count: int32 [256], P('tm'), may hold values from 1 to 64
Outputs:
- filtered: float32 [256, 256, 128], P('tm', 'row')
- smoothed: float32 [256, 256, 128], P('tm', 'row')
The draws below stay inside these ranges and needn't reach their ends.
Inputs may be any that keep to these rules, and one draw needn't show every extreme that they name: The live slots of an hour are its first obs_count ones.
All inputs are finite; a program needn't handle non-finite values.
Results may differ from the reference program's by a relative error of at most 0.0003.
Values sent between devices are 32-bit elements; how exact they have to be, the bound alone decides.
A program may use at most 192 MiB of HBM per device.

```python
import math
import jax
import jax.numpy as jnp
from jax import lax

NS = 256
NSITE = 128
SAMPLES = 128
TB_DEV = 2
SLOTS = 64
TOTAL_HOURS = 256


def decay_table(key, fast_share):
    child_keys = jax.random.split(key, 6)
    fast_mask = jax.random.uniform(child_keys[0], (NS,)) < fast_share
    slow_rate = jnp.exp(jax.random.uniform(child_keys[1], (NS,), minval=math.log(0.02 / TOTAL_HOURS), maxval=math.log(0.4 / TOTAL_HOURS)))
    fast_rate = jnp.exp(jax.random.uniform(child_keys[2], (NS,), minval=math.log(1.0 / 50), maxval=math.log(1.0 / 30)))
    rate_base = jnp.where(fast_mask, fast_rate, slow_rate)
    damping_factor = jnp.exp(jax.random.uniform(child_keys[3], (TOTAL_HOURS // TB_DEV, 1, NS), minval=math.log(0.5), maxval=math.log(2.0)))
    every_rate = jnp.broadcast_to(damping_factor * rate_base, (TOTAL_HOURS // TB_DEV, TB_DEV, NS)).reshape(TOTAL_HOURS, NS)
    gust_mask = jax.random.uniform(child_keys[4], (TOTAL_HOURS, 1)) < 3.0 / TOTAL_HOURS
    gust_dropout = jax.random.uniform(child_keys[5], (TOTAL_HOURS, 1), minval=0.5, maxval=0.8)
    return (jnp.exp(-every_rate) * jnp.where(gust_mask, gust_dropout, 1.0)).astype(jnp.float32)


def draw_decay_fwd(key, part):
    key = jax.random.fold_in(key, 11)
    return decay_table(key, 4.0 / NS)


def draw_decay_bwd(key, part):
    key = jax.random.fold_in(key, 23)
    return decay_table(key, 4.0 / NS)


def place_ends(result, own_key, smallest, top_value):
    longest = result.shape.index(max(result.shape))
    spots = []
    for shift in (0, 1):
        where = [jax.random.randint(jax.random.fold_in(own_key, axis), (), 0, length) for axis, length in enumerate(result.shape)]
        where[longest] = (where[longest] + shift) % result.shape[longest]
        spots.append(tuple(where))
    return result.at[spots[0]].set(smallest).at[spots[1]].set(top_value)


def levels(own_key, shape, cuts, smallest, top_value):
    level, own = 1.0, jax.random.fold_in(own_key, 6)
    for position, blocks in cuts:
        heights = jnp.exp(jax.random.uniform(jax.random.fold_in(own, position), (blocks,), jnp.float32, smallest / len(cuts), top_value / len(cuts)))
        level = level * jnp.repeat(heights, shape[position] // blocks).reshape([-1 if axis == position else 1 for axis in range(len(shape))])
    return level


def normal_values(own_key, shape, deviation, bound, cuts=(), kind=jnp.bfloat16):
    entries = jax.random.normal(own_key, shape, jnp.float32) * deviation
    if len(cuts) > 0:
        entries = levels(own_key, shape, cuts, -0.22, 0.18) * entries
    return jnp.clip(entries, min=-bound, max=bound).astype(kind)


def setup_inputs(seed: int = 0) -> dict:
    streams_of = jax.random.split(jax.random.key(seed), 8)
    decay_fwd = draw_decay_fwd(jax.random.fold_in(streams_of[7], 71), 0)
    decay_bwd = draw_decay_bwd(jax.random.fold_in(streams_of[7], 71), 0)
    angle = jnp.clip(0.2 + 0.3 * jax.random.uniform(streams_of[2], (TOTAL_HOURS,), jnp.float32) ** levels(streams_of[2], (TOTAL_HOURS,), ((0, 128),), -0.2, 0.2), 0.2, 0.5)
    gain = jnp.clip(jnp.exp(math.log(0.1) - 1.609438 * jax.random.uniform(streams_of[3], (TOTAL_HOURS, NS), jnp.float32) ** levels(streams_of[3], (TOTAL_HOURS, NS), ((0, 128),), -0.2, 0.2)), 0.02, 0.1)
    obs_values = normal_values(streams_of[4], (TOTAL_HOURS, SLOTS, SAMPLES), 1.0, 6.0, ((0, 128),), jnp.float32)
    obs_sites = place_ends(jax.random.randint(streams_of[5], (TOTAL_HOURS, SLOTS), 0, NSITE), jax.random.fold_in(streams_of[5], 1), 0, NSITE - 1).astype(jnp.int32)
    obs_count = place_ends(jax.random.randint(streams_of[6], (TOTAL_HOURS,), 1, SLOTS + 1), jax.random.fold_in(streams_of[6], 1), 1, SLOTS).astype(jnp.int32)
    return dict(decay_fwd=decay_fwd, decay_bwd=decay_bwd, angle=angle, gain=gain, obs_values=obs_values, obs_sites=obs_sites, obs_count=obs_count)


PRECISE = lax.Precision.HIGHEST

def hadamard(order):
    iota_index = jnp.arange(order, dtype=jnp.int32)
    parity = jnp.zeros((order, order), jnp.int32)
    for bit_level in range(order.bit_length() - 1):
        column_bit = iota_index[:, None] // 2 ** bit_level % 2
        row_bit = iota_index[None, :] // 2 ** bit_level % 2
        parity = parity + column_bit * row_bit
    return (1 - 2 * (parity % 2)).astype(jnp.float32) / math.sqrt(order)

def rotate_left(operand, hadamard_mat, cosine, sine_val):
    half_rows = operand.shape[-2] // 2
    upper_part = operand[..., :half_rows, :]
    lower_part = operand[..., half_rows:, :]
    coupled = jnp.concatenate([-jnp.matmul(hadamard_mat, lower_part, precision=PRECISE), jnp.matmul(hadamard_mat, upper_part, precision=PRECISE)], axis=-2)
    return cosine * operand + sine_val * coupled

def reference(decay_fwd, decay_bwd, angle, gain, obs_values, obs_sites, obs_count):
    hadamard_mat = hadamard(NSITE)
    slot_index = jnp.arange(SLOTS, dtype=jnp.int32)
    site_index = jnp.arange(NSITE, dtype=jnp.int32)

    def forward(carried_state, inputs):
        decay_now, angle_now, weight, values, site_ids, live_count = inputs
        site_table = ((site_ids[:, None] == site_index[None, :]) & (slot_index < live_count)[:, None]).astype(jnp.float32)
        site_sums = jnp.dot(site_table.T, values, precision=PRECISE, preferred_element_type=jnp.float32)
        source = weight[:, None] * jnp.concatenate([site_sums, site_sums], axis=0)
        carried_state = decay_now[:, None] * rotate_left(carried_state, hadamard_mat, jnp.cos(angle_now), jnp.sin(angle_now)) + source
        return (carried_state, (carried_state, source))
    initial = jnp.zeros((NS, SAMPLES), jnp.float32)
    final_state, (filtered, sources) = lax.scan(forward, initial, (decay_fwd, angle, gain, obs_values, obs_sites, obs_count))

    def backward(later_state, inputs):
        decay_now, angle_now, current, following = inputs
        smooth = current + decay_now[:, None] * rotate_left(later_state - following, hadamard_mat, jnp.cos(angle_now), -jnp.sin(angle_now))
        return (smooth, smooth)
    predicted = filtered[1:] - sources[1:]
    first_state, earlier = lax.scan(backward, filtered[-1], (decay_bwd[:-1], angle[:-1], filtered[:-1], predicted), reverse=True)
    smoothed = jnp.concatenate([earlier, filtered[-1:]], axis=0)
    return (filtered, smoothed)
```

```python
import functools
import math

import jax
import jax.numpy as jnp
from jax import lax
from jax.experimental import pallas as pl
from jax.experimental.pallas import tpu as pltpu
from jax.sharding import PartitionSpec as P

MESH = pl.DeviceIdType.MESH
F32 = jnp.float32
BF16 = jnp.bfloat16
HALF = 64
TILE = 16
LANES = 128


def split(x):
    high = x.astype(BF16)
    low = (x - high.astype(F32)).astype(BF16)
    return high, low


def times_signs(x, signs):
    rows = x.shape[0]
    high, low = split(x)
    both = jnp.dot(jnp.concatenate([high, low], axis=0), signs, preferred_element_type=F32)
    return both[:rows] + both[rows:]


def product(x, y):
    x_high, x_low = split(x)
    y_high, y_low = split(y)
    rows = x.shape[0]
    both = jnp.dot(jnp.concatenate([x_high, x_low], axis=0), y_high, preferred_element_type=F32)
    return both[:rows] + (both[rows:] + jnp.dot(x_high, y_low, preferred_element_type=F32))


def sign_matrix():
    shared = lax.broadcasted_iota(jnp.int32, (LANES, LANES), 0) & lax.broadcasted_iota(
        jnp.int32, (LANES, LANES), 1
    )
    for shift in (4, 2, 1):
        shared = shared ^ (shared >> shift)
    return (1 - 2 * (shared & 1)).astype(F32).astype(BF16)


def kernel(
    fwd_ref,
    bwd_ref,
    angle_ref,
    gain_ref,
    values_ref,
    sites_ref,
    count_ref,
    filtered_ref,
    smoothed_ref,
    outbox,
    inbox,
    history,
    before,
    final,
    ends,
    signs_ref,
    source_ref,
    start_ref,
    mine_ref,
    theirs_ref,
    send_sem,
    recv_sem,
    ready_sem,
):
    row = lax.axis_index("row")
    tm = lax.axis_index("tm")
    place = tm + row * (2 * HALF - 1 - 2 * tm)
    group = place // HALF
    me = place % HALF

    def device(a_place):
        return (a_place + row * (2 * HALF - 1 - 2 * a_place), row)

    other_core = (tm, 1 - row)

    barrier = pltpu.get_barrier_semaphore()

    def greet(k, carry):
        peer = (me + k) % HALF
        pl.semaphore_signal(
            barrier, inc=1, device_id=device(group * HALF + peer), device_id_type=MESH
        )
        return carry

    lax.fori_loop(1, HALF, greet, 0)
    pl.semaphore_signal(barrier, inc=1, device_id=other_core, device_id_type=MESH)

    @pl.when(group == 0)
    def _():
        pl.semaphore_signal(barrier, inc=1, device_id=device(HALF + me), device_id_type=MESH)

    signs = sign_matrix()
    signs_ref[...] = signs
    slot_ids = lax.broadcasted_iota(jnp.int32, (LANES, 64), 1)
    site_ids = lax.broadcasted_iota(jnp.int32, (LANES, 64), 0)
    forward = (row == 0).astype(F32)
    keep, turn = [], []
    for p in range(2):
        hour = p + row * (1 - 2 * p)
        decay = forward * fwd_ref[pl.ds(hour, 1), :] + (1.0 - forward) * bwd_ref[pl.ds(hour, 1), :]
        angle = jnp.full((1, 2 * LANES), angle_ref[hour], F32)
        keep.append(decay * jnp.cos(angle))
        turn.append(decay * jnp.sin(angle) * ((2.0 * forward - 1.0) / math.sqrt(LANES)))
        table = (
            (site_ids == sites_ref[pl.ds(hour, 1), :]) & (slot_ids < count_ref[hour])
        ).astype(F32).astype(BF16)
        values = values_ref[hour]
        first = values.astype(BF16)
        rest = values - first.astype(F32)
        second = rest.astype(BF16)
        third = (rest - second.astype(F32)).astype(BF16)
        sums = jnp.dot(
            table, jnp.concatenate([first, second, third], axis=1), preferred_element_type=F32
        )
        sums = sums[:, :LANES] + (sums[:, LANES : 2 * LANES] + sums[:, 2 * LANES :])
        sums = sums.T
        gain = gain_ref[pl.ds(hour, 1), :]
        for h in range(2):
            part = sums * gain[:, h * LANES : (h + 1) * LANES]
            source_ref[p, :, pl.ds(h * LANES, LANES)] = part
            outbox[pl.ds(8 * h + 2 * p, HALF, stride=TILE), :] = part[:HALF]
            outbox[pl.ds(8 * h + 2 * p + 1, HALF, stride=TILE), :] = part[HALF:]
            for at, coef in ((4, keep), (6, turn)):
                outbox[pl.ds(8 * h + at + p, HALF, stride=TILE), :] = jnp.broadcast_to(
                    coef[p][:, h * LANES : (h + 1) * LANES], (HALF, LANES)
                )

    pl.semaphore_wait(barrier, HALF + group)

    @pl.when(group == 1)
    def _():
        pl.semaphore_signal(ready_sem, inc=1, device_id=device(me), device_id_type=MESH)

    def slot(ref, k):
        return ref.at[pl.ds(pl.multiple_of(k * TILE, TILE), TILE), :]

    def to_peer(src, dst, peer, which):
        return pltpu.make_async_remote_copy(
            src_ref=src,
            dst_ref=dst,
            send_sem=send_sem.at[which],
            recv_sem=recv_sem.at[which],
            device_id=device(peer),
            device_id_type=MESH,
        )

    def hand_out(k, carry):
        peer = (me + k) % HALF
        to_peer(slot(outbox, peer), slot(inbox, me), group * HALF + peer, 0).start()
        return carry

    lax.fori_loop(1, HALF, hand_out, 0)
    mine = pl.ds(pl.multiple_of(me * TILE, TILE), TILE)
    inbox[mine, :] = outbox[mine, :]

    def all_but_own(ref, which):
        part = ref.at[pl.ds(0, (HALF - 1) * TILE), :]
        return to_peer(part, part, place, which)

    all_but_own(inbox, 0).wait_recv()

    tile_row = lax.broadcasted_iota(jnp.int32, (8, LANES), 0)
    tile_lane = lax.broadcasted_iota(jnp.int32, (8, LANES), 1)
    is_sample = tile_row < 2
    upper = ((tile_row == 2) & (tile_lane == me)) | ((tile_row == 3) & (tile_lane == me + HALF))
    lower = ((tile_row == 4) & (tile_lane == me)) | ((tile_row == 5) & (tile_lane == me + HALF))

    def block(b, u, l):
        rows_u = pl.ds(pl.multiple_of(b * TILE, 8), 8)
        rows_l = pl.ds(pl.multiple_of(b * TILE + 8, 8), 8)
        history[rows_u, :] = u
        history[rows_l, :] = l
        tile_u = inbox[rows_u, :]
        tile_l = inbox[rows_l, :]
        for p in range(2):
            from_u = times_signs(u, signs_ref[...])
            from_l = times_signs(l, signs_ref[...])
            source_u = tile_u if p == 0 else pltpu.roll(tile_u, 6, 0)
            source_l = tile_l if p == 0 else pltpu.roll(tile_l, 6, 0)
            u = (
                tile_u[4 + p : 5 + p] * u + jnp.where(is_sample, source_u, 0.0)
            ) - tile_u[6 + p : 7 + p] * from_l
            l = (
                tile_l[4 + p : 5 + p] * l + jnp.where(is_sample, source_l, 0.0)
            ) + tile_l[6 + p : 7 + p] * from_u
        return u, l

    chunk = 8

    def run(c, carried):
        u, l = carried
        for k in range(chunk):
            u, l = block(c * chunk + k, u, l)

        def pass_on(k, carry):
            b = c * chunk + k

            @pl.when(b != me)
            def _():
                to_peer(slot(history, b), slot(before, me), group * HALF + b, 1).start()

            return carry

        lax.fori_loop(0, chunk, pass_on, 0)
        return u, l

    u, l = lax.fori_loop(0, HALF // chunk, run, (upper.astype(F32), lower.astype(F32)))
    before[mine, :] = history[mine, :]
    final[:8, :] = u
    final[8:, :] = l

    @pl.when(group == 0)
    def _():
        pl.semaphore_wait(ready_sem, 1)

        def conclude(k, carry):
            peer = (me + k) % HALF
            to_peer(final, slot(ends, me), HALF + peer, 2).start()
            return carry

        lax.fori_loop(0, HALF, conclude, 0)

    def gathered(ref, at):
        return jnp.concatenate(
            [ref[pl.ds(at + 8 * h, HALF, stride=TILE), :] for h in range(2)], axis=1
        )

    all_but_own(before, 1).wait_recv()
    start_ref[:HALF, :] = gathered(before, 0)
    start_ref[HALF:, :] = gathered(before, 1)

    @pl.when(group == 1)
    def _():
        to_peer(ends, ends, place, 2).wait_recv()
        transfer = jnp.concatenate([gathered(before, 2 + i) for i in range(4)], axis=0)
        entry = jnp.concatenate([gathered(ends, 0), gathered(ends, 1)], axis=0)
        start_ref[...] += product(entry, transfer)

    state_u = start_ref[:, :LANES]
    state_l = start_ref[:, LANES:]
    swaps = []
    for p in range(2):
        hour = p + row * (1 - 2 * p)
        from_u = times_signs(state_u, signs)
        from_l = times_signs(state_l, signs)
        bare_u = keep[p][:, :LANES] * state_u - turn[p][:, :LANES] * from_l
        bare_l = keep[p][:, LANES:] * state_l + turn[p][:, LANES:] * from_u
        state_u = bare_u + source_ref[p, :, :LANES]
        state_l = bare_l + source_ref[p, :, LANES:]
        mine_ref[0, hour] = jnp.where(row == 0, state_u, bare_l)
        mine_ref[1, hour] = jnp.where(row == 0, state_l, bare_u)
        swap = pltpu.make_async_remote_copy(
            src_ref=mine_ref.at[1, hour],
            dst_ref=theirs_ref.at[hour],
            send_sem=send_sem.at[3 + p],
            recv_sem=recv_sem.at[3 + hour],
            device_id=other_core,
            device_id_type=MESH,
        )
        swap.start()
        swaps.append(swap)

    for hour in range(2):
        pltpu.make_async_remote_copy(
            src_ref=theirs_ref.at[hour],
            dst_ref=theirs_ref.at[hour],
            send_sem=send_sem.at[3],
            recv_sem=recv_sem.at[3 + hour],
            device_id=other_core,
            device_id_type=MESH,
        ).wait_recv()
        own = mine_ref[0, hour]
        their = theirs_ref[hour]
        filtered_ref[hour] = jnp.where(row == 0, own, their).T
        smoothed_ref[hour] = (own + their).T

    all_but_own(outbox, 0).wait_send()
    all_but_own(history, 1).wait_send()

    @pl.when(group == 0)
    def _():
        to_peer(ends, ends, place, 2).wait_send()

    for swap in swaps:
        swap.wait_send()


def local(decay_fwd, decay_bwd, angle, gain, obs_values, obs_sites, obs_count):
    vmem = pl.BlockSpec(memory_space=pltpu.VMEM)
    smem = pl.BlockSpec(memory_space=pltpu.SMEM)
    out = jax.ShapeDtypeStruct((2, LANES, LANES), F32)
    box = pltpu.VMEM((HALF * TILE, LANES), F32)
    return pl.pallas_call(
        kernel,
        out_shape=(out, out),
        in_specs=[vmem, vmem, smem, vmem, vmem, vmem, smem],
        out_specs=(vmem, vmem),
        scratch_shapes=[
            box,
            box,
            box,
            box,
            pltpu.VMEM((TILE, LANES), F32),
            box,
            pltpu.VMEM((LANES, LANES), BF16),
            pltpu.VMEM((2, LANES, 2 * LANES), F32),
            pltpu.VMEM((LANES, 2 * LANES), F32),
            pltpu.VMEM((2, 2, LANES, LANES), F32),
            pltpu.VMEM((2, LANES, LANES), F32),
            pltpu.SemaphoreType.DMA((5,)),
            pltpu.SemaphoreType.DMA((5,)),
            pltpu.SemaphoreType.REGULAR,
        ],
        compiler_params=pltpu.CompilerParams(
            collective_id=1, has_side_effects=True, vmem_limit_bytes=32 * 2**20
        ),
        name="smoother",
    )(decay_fwd, decay_bwd, angle, gain, obs_values, obs_sites, obs_count)


def solution(mesh):
    return jax.shard_map(
        local,
        mesh=mesh,
        in_specs=(
            P("tm", None),
            P("tm", None),
            P("tm"),
            P("tm", None),
            P("tm", None, None),
            P("tm", None),
            P("tm"),
        ),
        out_specs=(P("tm", "row", None), P("tm", "row", None)),
        check_vma=False,
    )
```

```python
import math

import jax
import jax.numpy as jnp
from jax import lax
from jax.experimental import pallas as pl
from jax.experimental.pallas import tpu as pltpu
from jax.sharding import PartitionSpec as P

MESH = pl.DeviceIdType.MESH
F32 = jnp.float32
BF16 = jnp.bfloat16
HALF = 64
CHUNK = 8
TILE = 16
LANES = 128
WHOLE = (2, 12)
SAMPLES = (6, 4)


def split(x):
    high = x.astype(BF16)
    low = (x - high.astype(F32)).astype(BF16)
    return high, low


def dot(x, y):
    return jnp.dot(x, y, preferred_element_type=F32)


def times_signs(x, signs_twice):
    return dot(jnp.concatenate(split(x), axis=1), signs_twice)


def sign_matrix():
    shared = lax.broadcasted_iota(jnp.int32, (LANES, LANES), 0) & lax.broadcasted_iota(
        jnp.int32, (LANES, LANES), 1
    )
    for shift in (4, 2, 1):
        shared = shared ^ (shared >> shift)
    return (1 - 2 * (shared & 1)).astype(F32).astype(BF16)


def kernel(
    fwd_hbm,
    bwd_hbm,
    angle_hbm,
    gain_hbm,
    values_hbm,
    sites_hbm,
    count_hbm,
    filtered_ref,
    smoothed_ref,
    fwd_ref,
    bwd_ref,
    angle_ref,
    gain_ref,
    values_ref,
    sites_ref,
    count_ref,
    outbox,
    inbox,
    history,
    before,
    final,
    ends,
    signs_ref,
    source_ref,
    start_ref,
    mine_ref,
    theirs_ref,
    load_sem,
    send_sem,
    recv_sem,
    inbox_sem,
    ready_sem,
):
    loads = [
        pltpu.make_async_copy(src, dst, load_sem.at[i])
        for i, (src, dst) in enumerate(
            (
                (values_hbm, values_ref),
                (sites_hbm, sites_ref),
                (count_hbm, count_ref),
                (fwd_hbm, fwd_ref),
                (bwd_hbm, bwd_ref),
                (gain_hbm, gain_ref),
                (angle_hbm, angle_ref),
            )
        )
    ]
    for load in loads:
        load.start()

    row = lax.axis_index("row")
    tm = lax.axis_index("tm")
    place = tm + row * (2 * HALF - 1 - 2 * tm)
    group = place >> 6
    me = place & 63
    my_x, my_y, my_z = me >> 5, (me >> 3) & 3, me & 7

    def device(a_place):
        return (a_place + row * (2 * HALF - 1 - 2 * a_place), row)

    other_core = (tm, 1 - row)

    def ranked(k, x_step):
        by_z, by_y = k >> 3, (k >> 1) & 3
        z = my_z + 4 + ((by_z + 1) >> 1) * (2 * (by_z & 1) - 1)
        y = my_y + 2 + ((by_y + 1) >> 1) * (2 * (by_y & 1) - 1)
        x = my_x + x_step
        return ((x & 1) << 5) + ((y & 3) << 3) + (z & 7)

    def ranked_peer(k):
        return ranked(k, 1 - (k & 1))

    barrier = pltpu.get_barrier_semaphore()

    def greet(k, carry):
        pl.semaphore_signal(
            barrier,
            inc=1,
            device_id=device(group * HALF + ranked_peer(k)),
            device_id_type=MESH,
        )
        return carry

    lax.fori_loop(0, HALF - 1, greet, 0)
    pl.semaphore_signal(barrier, inc=1, device_id=other_core, device_id_type=MESH)

    @pl.when(group == 0)
    def _():
        pl.semaphore_signal(barrier, inc=1, device_id=device(HALF + me), device_id_type=MESH)

    signs = sign_matrix()
    signs_twice = jnp.concatenate([signs, signs], axis=0)
    signs_ref[...] = signs_twice
    slot_ids = lax.broadcasted_iota(jnp.int32, (LANES, 64), 1)
    site_ids = lax.broadcasted_iota(jnp.int32, (LANES, 64), 0)
    forward = (row == 0).astype(F32)
    for load in loads:
        load.wait()
    keep, turn, source = [], [], []
    for p in range(2):
        hour = p + row * (1 - 2 * p)
        decay = forward * fwd_ref[pl.ds(hour, 1), :] + (1.0 - forward) * bwd_ref[pl.ds(hour, 1), :]
        angle = jnp.full((1, 2 * LANES), angle_ref[hour], F32)
        kept = decay * jnp.cos(angle)
        turned = decay * jnp.sin(angle) * ((2.0 * forward - 1.0) / math.sqrt(LANES))
        keep.append((kept[:, :LANES], kept[:, LANES:]))
        turn.append((-turned[:, :LANES], turned[:, LANES:]))
        table = (
            (site_ids == sites_ref[pl.ds(hour, 1), :]) & (slot_ids < count_ref[hour])
        ).astype(F32).astype(BF16)
        values = values_ref[hour]
        first = values.astype(BF16)
        rest = values - first.astype(F32)
        second = rest.astype(BF16)
        third = (rest - second.astype(F32)).astype(BF16)
        sums = dot(table, jnp.concatenate([first, second, third], axis=1))
        sums = sums[:, :LANES] + (sums[:, LANES : 2 * LANES] + sums[:, 2 * LANES :])
        sums = sums.T
        gain = gain_ref[pl.ds(hour, 1), :]
        source.append((sums * gain[:, :LANES], sums * gain[:, LANES:]))
        for h in range(2):
            source_ref[p, h] = source[p][h]

    def put(at, rows):
        outbox[pl.ds(at, HALF, stride=TILE), :] = jnp.broadcast_to(rows, (HALF, LANES))

    for h in range(2):
        both = (
            keep[1][h] * source[0][h]
            + turn[1][h] * times_signs(source[0][1 - h], signs_twice)
            + source[1][h]
        )
        for s in range(2):
            put(6 + 2 * h + s, both[s * HALF : (s + 1) * HALF])
        for p in range(2):
            put(2 + 8 * h + 2 * p, keep[p][h])
            put(3 + 8 * h + 2 * p, turn[p][h])

    pl.semaphore_wait(barrier, HALF + group)

    @pl.when(group == 1)
    def _():
        pl.semaphore_signal(ready_sem, inc=1, device_id=device(me), device_id_type=MESH)

    def slot(ref, k, part):
        return ref.at[pl.ds(k * TILE + part[0], part[1]), :]

    def to_peer(src, dst, peer, send, recv):
        return pltpu.make_async_remote_copy(
            src_ref=src,
            dst_ref=dst,
            send_sem=send,
            recv_sem=recv,
            device_id=device(peer),
            device_id_type=MESH,
        )

    def hand_out(k, carry):
        peer = ranked_peer(k)
        to_peer(
            slot(outbox, peer, WHOLE),
            slot(inbox, me, WHOLE),
            group * HALF + peer,
            send_sem.at[0],
            inbox_sem.at[me >> 3],
        ).start()
        return carry

    lax.fori_loop(0, HALF - 1, hand_out, 0)
    mine = pl.ds(pl.multiple_of(me * TILE, TILE), TILE)
    inbox[mine, :] = outbox[mine, :]

    def bulk(ref, count, part, send, recv):
        rows = ref.at[pl.ds(0, count * part[1]), :]
        return to_peer(rows, rows, place, send, recv)

    def chunk_arrived(c):
        @pl.when(c == me >> 3)
        def _():
            bulk(inbox, CHUNK - 1, WHOLE, send_sem.at[0], inbox_sem.at[c]).wait_recv()

        @pl.when(c != me >> 3)
        def _():
            bulk(inbox, CHUNK, WHOLE, send_sem.at[0], inbox_sem.at[c]).wait_recv()

    tile_row = lax.broadcasted_iota(jnp.int32, (8, LANES), 0)
    tile_lane = lax.broadcasted_iota(jnp.int32, (8, LANES), 1)
    upper = ((tile_row == 2) & (tile_lane == me)) | ((tile_row == 3) & (tile_lane == me + HALF))
    lower = ((tile_row == 4) & (tile_lane == me)) | ((tile_row == 5) & (tile_lane == me + HALF))

    def coefficients(b):
        upper_rows = inbox[pl.ds(pl.multiple_of(b * TILE, 8), 8), :]
        lower_rows = inbox[pl.ds(pl.multiple_of(b * TILE + 8, 8), 8), :]
        return upper_rows, lower_rows

    def twice_turned(b):
        upper_rows, lower_rows = coefficients(b)
        weights = []
        for rows in (lower_rows, upper_rows):
            high, low = split(rows[3:4])
            left = jnp.concatenate(
                [signs_ref[:LANES, :] * high, signs_ref[:LANES, :] * low], axis=1
            )
            weights.append(split(dot(left, signs_ref[...])))
        return weights

    def block(b, x, weights):
        tile_u, tile_l = coefficients(b)

        def spread(at):
            return tile_u[at : at + 1], tile_l[at : at + 1]

        (keep_u, keep_l), (turn_u, turn_l) = spread(2), spread(3)
        (next_keep_u, next_keep_l), (next_turn_u, next_turn_l) = spread(4), spread(5)
        high, low = split(x)
        turned = dot(jnp.concatenate([high, low], axis=1), signs_ref[...])
        kept = jnp.concatenate([keep_u * x[:8], keep_l * x[8:]], axis=0)
        kept_turned = times_signs(kept, signs_ref[...])
        parts = jnp.concatenate([high, low, high], axis=1)
        both_u, both_l = [
            dot(parts, jnp.concatenate([w_high, w_high, w_low], axis=0))
            for w_high, w_low in weights
        ]
        source_u = jnp.where(tile_row >= 6, tile_u, 0.0)
        source_l = jnp.where(tile_row >= 6, pltpu.roll(tile_l, 6, 0), 0.0)
        u = (
            (next_keep_u * kept[:8] + source_u)
            + (next_keep_u * turn_u) * turned[8:]
            + next_turn_u * (kept_turned[8:] + both_u[:8])
        )
        l = (
            (next_keep_l * kept[8:] + source_l)
            + (next_keep_l * turn_l) * turned[:8]
            + next_turn_l * (kept_turned[:8] + both_l[8:])
        )
        return jnp.concatenate([u, l], axis=0)

    def keep_state(ref, at, x):
        ref[pl.ds(pl.multiple_of(at, TILE), 8), :] = x[:8]
        ref[pl.ds(at + 8, 2), :] = x[14:]
        ref[pl.ds(at + 10, 4), :] = x[10:14]

    def run(part):
        def run_chunk(c, carried):
            x, weights = carried

            @pl.when(c < HALF // CHUNK - 1)
            def _():
                chunk_arrived(c + 1)

            for k in range(CHUNK):
                b = c * CHUNK + k
                keep_state(history, b * TILE, x)
                own = (b == me).astype(jnp.int32)
                peer = b + own * (me + 1 - 2 * (me & 1) - b)
                to_peer(
                    slot(history, b, part),
                    slot(before, me + own * (HALF - me), part),
                    group * HALF + peer,
                    send_sem.at[1],
                    recv_sem.at[1],
                ).start()
                following = twice_turned(jnp.minimum(b + 1, HALF - 1))
                x = block(b, x, weights)
                weights = following
            return x, weights

        chunk_arrived(0)
        x = jnp.concatenate([upper.astype(F32), lower.astype(F32)], axis=0)
        x, _ = lax.fori_loop(0, HALF // CHUNK, run_chunk, (x, twice_turned(0)))
        keep_state(final, 0, x)

    @pl.when(group == 0)
    def _():
        run(SAMPLES)
        pl.semaphore_wait(ready_sem, 1)

        def conclude(k, carry):
            peer = ranked(k, k & 1)
            to_peer(
                slot(final, 0, SAMPLES),
                slot(ends, me, SAMPLES),
                HALF + peer,
                send_sem.at[2],
                recv_sem.at[2],
            ).start()
            return carry

        lax.fori_loop(0, HALF, conclude, 0)
        bulk(before, HALF, SAMPLES, send_sem.at[1], recv_sem.at[1]).wait_recv()

    @pl.when(group == 1)
    def _():
        run(WHOLE)
        bulk(before, HALF, WHOLE, send_sem.at[1], recv_sem.at[1]).wait_recv()

    before[mine, :] = history[mine, :]

    def gathered(ref, at):
        return ref[pl.ds(at, HALF, stride=TILE), :]

    for h in range(2):
        for s in range(2):
            start_ref[h, pl.ds(s * HALF, HALF), :] = gathered(before, 6 + 2 * h + s)

    @pl.when(group == 1)
    def _():
        transfer = jnp.concatenate(
            [
                jnp.concatenate([gathered(before, 2 + 8 * h + i) for h in range(2)], axis=1)
                for i in range(4)
            ],
            axis=0,
        )
        transfer_high, transfer_low = split(transfer)
        bulk(ends, HALF, SAMPLES, send_sem.at[2], recv_sem.at[2]).wait_recv()
        entry = jnp.concatenate(
            [
                jnp.concatenate([gathered(ends, 6 + 2 * h + s) for h in range(2)], axis=1)
                for s in range(2)
            ],
            axis=0,
        )
        entry_high, entry_low = split(entry)
        moved = dot(jnp.concatenate([entry_high, entry_low], axis=0), transfer_high)
        moved = moved[:LANES] + (moved[LANES:] + dot(entry_high, transfer_low))
        for h in range(2):
            start_ref[h] += moved[:, h * LANES : (h + 1) * LANES]

    state = [start_ref[0], start_ref[1]]
    swaps = []
    for p in range(2):
        hour = p + row * (1 - 2 * p)
        turned = times_signs(jnp.concatenate(state, axis=0), signs_ref[...])
        bare = [
            keep[p][0] * state[0] + turn[p][0] * turned[LANES:],
            keep[p][1] * state[1] + turn[p][1] * turned[:LANES],
        ]
        state = [bare[h] + source_ref[p, h] for h in range(2)]
        mine_ref[0, hour] = jnp.where(row == 0, state[0], bare[1])
        mine_ref[1, hour] = jnp.where(row == 0, state[1], bare[0])
        swap = pltpu.make_async_remote_copy(
            src_ref=mine_ref.at[1, hour],
            dst_ref=theirs_ref.at[hour],
            send_sem=send_sem.at[3 + p],
            recv_sem=recv_sem.at[3 + hour],
            device_id=other_core,
            device_id_type=MESH,
        )
        swap.start()
        swaps.append(swap)

    for hour in range(2):
        pltpu.make_async_remote_copy(
            src_ref=theirs_ref.at[hour],
            dst_ref=theirs_ref.at[hour],
            send_sem=send_sem.at[3],
            recv_sem=recv_sem.at[3 + hour],
            device_id=other_core,
            device_id_type=MESH,
        ).wait_recv()
        own = mine_ref[0, hour]
        their = theirs_ref[hour]
        filtered_ref[hour] = jnp.where(row == 0, own, their).T
        smoothed_ref[hour] = (own + their).T

    bulk(outbox, HALF - 1, WHOLE, send_sem.at[0], recv_sem.at[0]).wait_send()

    @pl.when(group == 0)
    def _():
        bulk(history, HALF, SAMPLES, send_sem.at[1], recv_sem.at[1]).wait_send()
        bulk(ends, HALF, SAMPLES, send_sem.at[2], recv_sem.at[2]).wait_send()

    @pl.when(group == 1)
    def _():
        bulk(history, HALF, WHOLE, send_sem.at[1], recv_sem.at[1]).wait_send()

    for swap in swaps:
        swap.wait_send()


def local(decay_fwd, decay_bwd, angle, gain, obs_values, obs_sites, obs_count):
    args = (decay_fwd, decay_bwd, angle, gain, obs_values, obs_sites, obs_count)
    vmem = pl.BlockSpec(memory_space=pltpu.VMEM)
    out = jax.ShapeDtypeStruct((2, LANES, LANES), F32)
    box = pltpu.VMEM((HALF * TILE, LANES), F32)
    return pl.pallas_call(
        kernel,
        out_shape=(out, out),
        in_specs=[pl.BlockSpec(memory_space=pl.ANY)] * len(args),
        out_specs=(vmem, vmem),
        scratch_shapes=[
            *(
                (pltpu.SMEM if arg.ndim == 1 else pltpu.VMEM)(arg.shape, arg.dtype)
                for arg in args
            ),
            box,
            box,
            box,
            pltpu.VMEM(((HALF + 1) * TILE, LANES), F32),
            pltpu.VMEM((TILE, LANES), F32),
            box,
            pltpu.VMEM((2 * LANES, LANES), BF16),
            pltpu.VMEM((2, 2, LANES, LANES), F32),
            pltpu.VMEM((2, LANES, LANES), F32),
            pltpu.VMEM((2, 2, LANES, LANES), F32),
            pltpu.VMEM((2, LANES, LANES), F32),
            pltpu.SemaphoreType.DMA((len(args),)),
            pltpu.SemaphoreType.DMA((5,)),
            pltpu.SemaphoreType.DMA((5,)),
            pltpu.SemaphoreType.DMA((HALF // CHUNK,)),
            pltpu.SemaphoreType.REGULAR,
        ],
        compiler_params=pltpu.CompilerParams(
            collective_id=1, has_side_effects=True, vmem_limit_bytes=60 * 2**20
        ),
        name="smoother",
    )(*args)


def solution(mesh):
    return jax.shard_map(
        local,
        mesh=mesh,
        in_specs=(
            P("tm", None),
            P("tm", None),
            P("tm"),
            P("tm", None),
            P("tm", None, None),
            P("tm", None),
            P("tm"),
        ),
        out_specs=(P("tm", "row", None), P("tm", "row", None)),
        check_vma=False,
    )
```

```python
import math

import jax
import jax.numpy as jnp
from jax import lax
from jax.experimental import pallas as pl
from jax.experimental.pallas import tpu as pltpu
from jax.sharding import PartitionSpec as P

MESH = pl.DeviceIdType.MESH
F32 = jnp.float32
BF16 = jnp.bfloat16
HALF = 64
CHUNK = 8
TILE = 16
LANES = 128
STATE = (2, 12)
INPUTS = (3, 9)
SAMPLES = (6, 4)


def split(x):
    high = x.astype(BF16)
    low = (x - high.astype(F32)).astype(BF16)
    return high, low


def dot(x, y):
    return jnp.dot(x, y, preferred_element_type=F32)


def times_signs(x, signs_twice):
    return dot(jnp.concatenate(split(x), axis=1), signs_twice)


def sign_matrix():
    shared = lax.broadcasted_iota(jnp.int32, (LANES, LANES), 0) & lax.broadcasted_iota(
        jnp.int32, (LANES, LANES), 1
    )
    for shift in (4, 2, 1):
        shared = shared ^ (shared >> shift)
    return (1 - 2 * (shared & 1)).astype(F32).astype(BF16)


def kernel(
    fwd_hbm,
    bwd_hbm,
    angle_hbm,
    gain_hbm,
    values_hbm,
    sites_hbm,
    count_hbm,
    own_ref,
    their_ref,
    fwd_ref,
    bwd_ref,
    angle_ref,
    gain_ref,
    values_ref,
    sites_ref,
    count_ref,
    outbox,
    inbox,
    history,
    before,
    final,
    ends,
    signs_ref,
    source_ref,
    start_ref,
    mine_ref,
    theirs_ref,
    load_sem,
    send_sem,
    recv_sem,
    inbox_sem,
    ready_sem,
):
    loads = [
        pltpu.make_async_copy(src, dst, load_sem.at[i])
        for i, (src, dst) in enumerate(
            (
                (values_hbm, values_ref),
                (sites_hbm, sites_ref),
                (count_hbm, count_ref),
                (fwd_hbm, fwd_ref),
                (bwd_hbm, bwd_ref),
                (gain_hbm, gain_ref),
                (angle_hbm, angle_ref),
            )
        )
    ]
    for load in loads:
        load.start()

    row = lax.axis_index("row")
    tm = lax.axis_index("tm")
    place = tm + row * (2 * HALF - 1 - 2 * tm)
    group = place >> 6
    me = place & 63
    my_x, my_y, my_z = me >> 5, (me >> 3) & 3, me & 7

    def device(a_place):
        return (a_place + row * (2 * HALF - 1 - 2 * a_place), row)

    other_core = (tm, 1 - row)

    def ranked(k, x_step):
        by_z, by_y = k >> 3, (k >> 1) & 3
        z = my_z + 4 + ((by_z + 1) >> 1) * (2 * (by_z & 1) - 1)
        y = my_y + 2 + ((by_y + 1) >> 1) * (2 * (by_y & 1) - 1)
        x = my_x + x_step
        return ((x & 1) << 5) + ((y & 3) << 3) + (z & 7)

    def ranked_peer(k):
        return ranked(k, 1 - (k & 1))

    barrier = pltpu.get_barrier_semaphore()

    def greet(k, carry):
        pl.semaphore_signal(
            barrier,
            inc=1,
            device_id=device(group * HALF + ranked_peer(k)),
            device_id_type=MESH,
        )
        return carry

    lax.fori_loop(0, HALF - 1, greet, 0)
    pl.semaphore_signal(barrier, inc=1, device_id=other_core, device_id_type=MESH)

    @pl.when(group == 0)
    def _():
        pl.semaphore_signal(barrier, inc=1, device_id=device(HALF + me), device_id_type=MESH)

    signs = sign_matrix()
    signs_twice = jnp.concatenate([signs, signs], axis=0)
    signs_ref[...] = signs_twice
    slot_ids = lax.broadcasted_iota(jnp.int32, (LANES, 64), 1)
    site_ids = lax.broadcasted_iota(jnp.int32, (LANES, 64), 0)
    forward = (row == 0).astype(F32)
    for load in loads:
        load.wait()
    keep, turn, source, decays, angles = [], [], [], [], []
    for p in range(2):
        hour = p + row * (1 - 2 * p)
        decay = forward * fwd_ref[pl.ds(hour, 1), :] + (1.0 - forward) * bwd_ref[pl.ds(hour, 1), :]
        angle = jnp.full((1, 2 * LANES), angle_ref[hour], F32)
        cosine = jnp.cos(angle)
        sine = jnp.sin(angle) * ((2.0 * forward - 1.0) / math.sqrt(LANES))
        kept = decay * cosine
        turned = decay * sine
        keep.append((kept[:, :LANES], kept[:, LANES:]))
        turn.append((-turned[:, :LANES], turned[:, LANES:]))
        decays.append((decay[:, :LANES], decay[:, LANES:]))
        angles += [cosine[:, :LANES], sine[:, :LANES]]
        table = (
            (site_ids == sites_ref[pl.ds(hour, 1), :]) & (slot_ids < count_ref[hour])
        ).astype(F32).astype(BF16)
        values = values_ref[hour]
        first = values.astype(BF16)
        rest = values - first.astype(F32)
        second = rest.astype(BF16)
        third = (rest - second.astype(F32)).astype(BF16)
        sums = dot(table, jnp.concatenate([first, second, third], axis=1))
        sums = sums[:, :LANES] + (sums[:, LANES : 2 * LANES] + sums[:, 2 * LANES :])
        sums = sums.T
        gain = gain_ref[pl.ds(hour, 1), :]
        source.append((sums * gain[:, :LANES], sums * gain[:, LANES:]))
        for h in range(2):
            source_ref[p, h] = source[p][h]

    def put(at, rows):
        outbox[pl.ds(at, HALF, stride=TILE), :] = jnp.broadcast_to(rows, (HALF, LANES))

    for h in range(2):
        both = (
            keep[1][h] * source[0][h]
            + turn[1][h] * times_signs(source[0][1 - h], signs_twice)
            + source[1][h]
        )
        for s in range(2):
            put(6 + 2 * h + s, both[s * HALF : (s + 1) * HALF])
        for p in range(2):
            put(4 + 6 * h + p, decays[p][h])
    quarter = lax.broadcasted_iota(jnp.int32, (1, LANES), 1) // 32
    packed = angles[0]
    for i in range(1, 4):
        packed = jnp.where(quarter == i, angles[i], packed)
    put(3, packed)

    pl.semaphore_wait(barrier, HALF + group)

    @pl.when(group == 1)
    def _():
        pl.semaphore_signal(ready_sem, inc=1, device_id=device(me), device_id_type=MESH)

    def slot(ref, k, part):
        return ref.at[pl.ds(k * TILE + part[0], part[1]), :]

    def to_peer(src, dst, peer, send, recv):
        return pltpu.make_async_remote_copy(
            src_ref=src,
            dst_ref=dst,
            send_sem=send,
            recv_sem=recv,
            device_id=device(peer),
            device_id_type=MESH,
        )

    def hand_out(k, carry):
        peer = ranked_peer(k)
        to_peer(
            slot(outbox, peer, INPUTS),
            slot(inbox, me, INPUTS),
            group * HALF + peer,
            send_sem.at[0],
            inbox_sem.at[me >> 3],
        ).start()
        return carry

    lax.fori_loop(0, HALF - 1, hand_out, 0)
    mine = pl.ds(pl.multiple_of(me * TILE, TILE), TILE)
    inbox[mine, :] = outbox[mine, :]

    def bulk(ref, count, part, send, recv):
        rows = ref.at[pl.ds(0, count * part[1]), :]
        return to_peer(rows, rows, place, send, recv)

    def chunk_arrived(c):
        @pl.when(c == me >> 3)
        def _():
            bulk(inbox, CHUNK - 1, INPUTS, send_sem.at[0], inbox_sem.at[c]).wait_recv()

        @pl.when(c != me >> 3)
        def _():
            bulk(inbox, CHUNK, INPUTS, send_sem.at[0], inbox_sem.at[c]).wait_recv()

    tile_row = lax.broadcasted_iota(jnp.int32, (8, LANES), 0)
    tile_lane = lax.broadcasted_iota(jnp.int32, (8, LANES), 1)
    upper = ((tile_row == 2) & (tile_lane == me)) | ((tile_row == 3) & (tile_lane == me + HALF))
    lower = ((tile_row == 4) & (tile_lane == me)) | ((tile_row == 5) & (tile_lane == me + HALF))

    def coefficients(b):
        upper_rows = inbox[pl.ds(pl.multiple_of(b * TILE, 8), 8), :]
        lower_rows = inbox[pl.ds(pl.multiple_of(b * TILE + 8, 8), 8), :]
        cosine, sine, next_cosine, next_sine = [
            jnp.broadcast_to(upper_rows[3:4, 32 * i : 32 * i + 1], (1, LANES)) for i in range(4)
        ]
        decay = upper_rows[4:5], lower_rows[2:3]
        next_decay = upper_rows[5:6], lower_rows[3:4]
        return (
            [d * cosine for d in decay],
            [-decay[0] * sine, decay[1] * sine],
            [d * next_cosine for d in next_decay],
            [-next_decay[0] * next_sine, next_decay[1] * next_sine],
            upper_rows,
            lower_rows,
        )

    def twice_turned(coefs):
        parts = []
        for turn_row in (coefs[1][1], coefs[1][0]):
            high, low = split(turn_row)
            left = jnp.concatenate(
                [signs_ref[:LANES, :] * high, signs_ref[:LANES, :] * low], axis=1
            )
            parts.append(split(dot(left, signs_ref[...])))
        (u_high, u_low), (l_high, l_low) = parts
        return jnp.concatenate(
            [
                jnp.concatenate([u_high, l_high], axis=1),
                jnp.concatenate([u_low, l_low], axis=1),
            ],
            axis=0,
        )

    def block(x, coefs, weights):
        keep_rows, turn_rows, next_keep, next_turn, tile_u, tile_l = coefs
        high, low = split(x)
        kept = jnp.concatenate([keep_rows[0] * x[:8], keep_rows[1] * x[8:]], axis=0)
        turned = dot(
            jnp.concatenate(
                [
                    jnp.concatenate([high, low], axis=1),
                    jnp.concatenate(split(kept), axis=1),
                ],
                axis=0,
            ),
            signs_ref[...],
        )
        both = dot(
            jnp.concatenate(
                [
                    jnp.concatenate([high, high], axis=1),
                    jnp.concatenate([low, jnp.zeros_like(low)], axis=1),
                ],
                axis=0,
            ),
            weights,
        )
        source_u = jnp.where(tile_row >= 6, tile_u, 0.0)
        source_l = jnp.where(tile_row >= 6, pltpu.roll(tile_l, 6, 0), 0.0)
        u = (
            (next_keep[0] * kept[:8] + source_u)
            + (next_keep[0] * turn_rows[0]) * turned[8:16]
            + next_turn[0] * (turned[24:] + (both[:8, :LANES] + both[16:24, :LANES]))
        )
        l = (
            (next_keep[1] * kept[8:] + source_l)
            + (next_keep[1] * turn_rows[1]) * turned[:8]
            + next_turn[1] * (turned[16:24] + (both[8:16, LANES:] + both[24:, LANES:]))
        )
        return jnp.concatenate([u, l], axis=0)

    def keep_state(ref, at, x):
        ref[pl.ds(pl.multiple_of(at, TILE), 8), :] = x[:8]
        ref[pl.ds(at + 8, 2), :] = x[14:]
        ref[pl.ds(at + 10, 4), :] = x[10:14]

    def run(part):
        def run_chunk(c, carried):
            x, weights = carried

            @pl.when(c < HALF // CHUNK - 1)
            def _():
                chunk_arrived(c + 1)

            def send(b):
                own = (b == me).astype(jnp.int32)
                peer = b + own * (me + 1 - 2 * (me & 1) - b)
                to_peer(
                    slot(history, b, part),
                    slot(before, me + own * (HALF - me), part),
                    group * HALF + peer,
                    send_sem.at[1],
                    recv_sem.at[1],
                ).start()

            for k in range(CHUNK):
                b = c * CHUNK + k
                keep_state(history, b * TILE, x)
                following = twice_turned(coefficients(jnp.minimum(b + 1, HALF - 1)))
                x = block(x, coefficients(b), weights)
                weights = following
                if k % 2 == 1:
                    send(b - 1)
                    send(b)
            return x, weights

        chunk_arrived(0)
        x = jnp.concatenate([upper.astype(F32), lower.astype(F32)], axis=0)
        x, _ = lax.fori_loop(0, HALF // CHUNK, run_chunk, (x, twice_turned(coefficients(0))))
        keep_state(final, 0, x)

    @pl.when(group == 0)
    def _():
        run(SAMPLES)
        pl.semaphore_wait(ready_sem, 1)

        def conclude(k, carry):
            peer = ranked(k, k & 1)
            to_peer(
                slot(final, 0, SAMPLES),
                slot(ends, me, SAMPLES),
                HALF + peer,
                send_sem.at[2],
                recv_sem.at[2],
            ).start()
            return carry

        lax.fori_loop(0, HALF, conclude, 0)
        bulk(before, HALF, SAMPLES, send_sem.at[1], recv_sem.at[1]).wait_recv()

    @pl.when(group == 1)
    def _():
        run(STATE)
        bulk(before, HALF, STATE, send_sem.at[1], recv_sem.at[1]).wait_recv()

    before[mine, :] = history[mine, :]

    def gathered(ref, at):
        return ref[pl.ds(at, HALF, stride=TILE), :]

    for h in range(2):
        for s in range(2):
            start_ref[h, pl.ds(s * HALF, HALF), :] = gathered(before, 6 + 2 * h + s)

    @pl.when(group == 1)
    def _():
        transfer = jnp.concatenate(
            [
                jnp.concatenate([gathered(before, 2 + 8 * h + i) for h in range(2)], axis=1)
                for i in range(4)
            ],
            axis=0,
        )
        transfer_high, transfer_low = split(transfer)
        bulk(ends, HALF, SAMPLES, send_sem.at[2], recv_sem.at[2]).wait_recv()
        entry = jnp.concatenate(
            [
                jnp.concatenate([gathered(ends, 6 + 2 * h + s) for h in range(2)], axis=1)
                for s in range(2)
            ],
            axis=0,
        )
        entry_high, entry_low = split(entry)
        moved = dot(jnp.concatenate([entry_high, entry_low], axis=0), transfer_high)
        moved = moved[:LANES] + (moved[LANES:] + dot(entry_high, transfer_low))
        for h in range(2):
            start_ref[h] += moved[:, h * LANES : (h + 1) * LANES]

    state = [start_ref[0], start_ref[1]]
    swaps = []
    for p in range(2):
        hour = p + row * (1 - 2 * p)
        turned = times_signs(jnp.concatenate(state, axis=0), signs_ref[...])
        bare = [
            keep[p][0] * state[0] + turn[p][0] * turned[LANES:],
            keep[p][1] * state[1] + turn[p][1] * turned[:LANES],
        ]
        state = [bare[h] + source_ref[p, h] for h in range(2)]
        mine_ref[0, hour] = jnp.where(row == 0, state[0], bare[1])
        mine_ref[1, hour] = jnp.where(row == 0, state[1], bare[0])
        swap = pltpu.make_async_remote_copy(
            src_ref=mine_ref.at[1, hour],
            dst_ref=theirs_ref.at[hour],
            send_sem=send_sem.at[3 + p],
            recv_sem=recv_sem.at[3 + hour],
            device_id=other_core,
            device_id_type=MESH,
        )
        swap.start()
        swaps.append(swap)

    for hour in range(2):
        pltpu.make_async_remote_copy(
            src_ref=theirs_ref.at[hour],
            dst_ref=theirs_ref.at[hour],
            send_sem=send_sem.at[3],
            recv_sem=recv_sem.at[3 + hour],
            device_id=other_core,
            device_id_type=MESH,
        ).wait_recv()
        own = mine_ref[0, hour]
        their = theirs_ref[hour]
        own_ref[hour] = own.T
        their_ref[hour] = their.T

    bulk(outbox, HALF - 1, INPUTS, send_sem.at[0], recv_sem.at[0]).wait_send()

    @pl.when(group == 0)
    def _():
        bulk(history, HALF, SAMPLES, send_sem.at[1], recv_sem.at[1]).wait_send()
        bulk(ends, HALF, SAMPLES, send_sem.at[2], recv_sem.at[2]).wait_send()

    @pl.when(group == 1)
    def _():
        bulk(history, HALF, STATE, send_sem.at[1], recv_sem.at[1]).wait_send()

    for swap in swaps:
        swap.wait_send()


def local(decay_fwd, decay_bwd, angle, gain, obs_values, obs_sites, obs_count):
    args = (decay_fwd, decay_bwd, angle, gain, obs_values, obs_sites, obs_count)
    vmem = pl.BlockSpec(memory_space=pltpu.VMEM)
    out = jax.ShapeDtypeStruct((2, LANES, LANES), F32)
    box = pltpu.VMEM((HALF * TILE, LANES), F32)
    own, their = pl.pallas_call(
        kernel,
        out_shape=(out, out),
        in_specs=[pl.BlockSpec(memory_space=pl.ANY)] * len(args),
        out_specs=(vmem, vmem),
        scratch_shapes=[
            *(
                (pltpu.SMEM if arg.ndim == 1 else pltpu.VMEM)(arg.shape, arg.dtype)
                for arg in args
            ),
            box,
            box,
            box,
            pltpu.VMEM(((HALF + 1) * TILE, LANES), F32),
            pltpu.VMEM((TILE, LANES), F32),
            box,
            pltpu.VMEM((2 * LANES, LANES), BF16),
            pltpu.VMEM((2, 2, LANES, LANES), F32),
            pltpu.VMEM((2, LANES, LANES), F32),
            pltpu.VMEM((2, 2, LANES, LANES), F32),
            pltpu.VMEM((2, LANES, LANES), F32),
            pltpu.SemaphoreType.DMA((len(args),)),
            pltpu.SemaphoreType.DMA((5,)),
            pltpu.SemaphoreType.DMA((5,)),
            pltpu.SemaphoreType.DMA((HALF // CHUNK,)),
            pltpu.SemaphoreType.REGULAR,
        ],
        compiler_params=pltpu.CompilerParams(
            collective_id=1, has_side_effects=True, vmem_limit_bytes=32 * 2**20
        ),
        name="smoother",
    )(*(pltpu.with_memory_space_constraint(arg, pltpu.HBM) for arg in args))
    return jnp.where(lax.axis_index("row") == 0, own, their), own + their


def solution(mesh):
    return jax.shard_map(
        local,
        mesh=mesh,
        in_specs=(
            P("tm", None),
            P("tm", None),
            P("tm"),
            P("tm", None),
            P("tm", None, None),
            P("tm", None),
            P("tm"),
        ),
        out_specs=(P("tm", "row", None), P("tm", "row", None)),
        check_vma=False,
    )
```

```python
import math

import jax
import jax.numpy as jnp
from jax import lax
from jax.experimental import pallas as pl
from jax.experimental.pallas import tpu as pltpu
from jax.sharding import PartitionSpec as P

MESH = pl.DeviceIdType.MESH
F32 = jnp.float32
BF16 = jnp.bfloat16
HALF = 64
CHUNK = 8
TILE = 16
LANES = 128
STATE = (2, 12)
SAMPLES = (6, 4)
SOURCES = (4, 4)
COEFS = (8, 5)


def split(x):
    high = x.astype(BF16)
    low = (x - high.astype(F32)).astype(BF16)
    return high, low


def dot(x, y):
    return jnp.dot(x, y, preferred_element_type=F32)


def times_signs(x, signs_twice):
    return dot(jnp.concatenate(split(x), axis=1), signs_twice)


def sign_matrix():
    shared = lax.broadcasted_iota(jnp.int32, (LANES, LANES), 0) & lax.broadcasted_iota(
        jnp.int32, (LANES, LANES), 1
    )
    for shift in (4, 2, 1):
        shared = shared ^ (shared >> shift)
    return (1 - 2 * (shared & 1)).astype(F32).astype(BF16)


def kernel(
    fwd_hbm,
    bwd_hbm,
    angle_hbm,
    gain_hbm,
    values_hbm,
    sites_hbm,
    count_hbm,
    own_ref,
    their_ref,
    fwd_ref,
    bwd_ref,
    angle_ref,
    gain_ref,
    values_ref,
    sites_ref,
    count_ref,
    outbox,
    own_coefs,
    line_sources,
    line_coefs,
    inbox,
    history,
    before,
    final,
    ends,
    signs_ref,
    source_ref,
    start_ref,
    mine_ref,
    theirs_ref,
    load_sem,
    send_sem,
    recv_sem,
    line_sem,
    inbox_sem,
    ready_sem,
):
    loads = [
        pltpu.make_async_copy(src, dst, load_sem.at[i])
        for i, (src, dst) in enumerate(
            (
                (values_hbm, values_ref),
                (sites_hbm, sites_ref),
                (count_hbm, count_ref),
                (fwd_hbm, fwd_ref),
                (bwd_hbm, bwd_ref),
                (gain_hbm, gain_ref),
                (angle_hbm, angle_ref),
            )
        )
    ]
    for load in loads:
        load.start()

    row = lax.axis_index("row")
    tm = lax.axis_index("tm")
    place = tm + row * (2 * HALF - 1 - 2 * tm)
    group = place >> 6
    me = place & 63
    my_x, my_y, my_z, my_line = me >> 5, (me >> 3) & 3, me & 7, me >> 3
    share = my_z * 8 + my_line

    def device(a_place):
        return (a_place + row * (2 * HALF - 1 - 2 * a_place), row)

    other_core = (tm, 1 - row)

    def ranked(k, x_step):
        by_z, by_y = k >> 3, (k >> 1) & 3
        z = my_z + 4 + ((by_z + 1) >> 1) * (2 * (by_z & 1) - 1)
        y = my_y + 2 + ((by_y + 1) >> 1) * (2 * (by_y & 1) - 1)
        x = my_x + x_step
        return ((x & 1) << 5) + ((y & 3) << 3) + (z & 7)

    line_mates = [(my_z + step) & 7 for step in (4, 5, 3, 6, 2, 7, 1)]
    plane_mates = [
        (((my_x + x_step) & 1) << 2) + ((my_y + y_step) & 3)
        for x_step, y_step in ((1, 2), (1, 1), (1, 3), (0, 2), (1, 0), (0, 1), (0, 3))
    ]

    def in_half(line, z):
        return device(group * HALF + line * 8 + z)

    barrier = pltpu.get_barrier_semaphore()

    def greet(target):
        pl.semaphore_signal(barrier, inc=1, device_id=target, device_id_type=MESH)

    for z in line_mates:
        greet(in_half(my_line, z))
    for line in plane_mates:
        greet(in_half(line, my_z))
    greet(other_core)

    @pl.when(group == 0)
    def _():
        greet(device(HALF + me))

    signs = sign_matrix()
    signs_twice = jnp.concatenate([signs, signs], axis=0)
    signs_ref[...] = signs_twice
    slot_ids = lax.broadcasted_iota(jnp.int32, (LANES, 64), 1)
    site_ids = lax.broadcasted_iota(jnp.int32, (LANES, 64), 0)
    forward = (row == 0).astype(F32)
    for load in loads:
        load.wait()
    keep, turn, source, decays, angles = [], [], [], [], []
    for p in range(2):
        hour = p + row * (1 - 2 * p)
        decay = forward * fwd_ref[pl.ds(hour, 1), :] + (1.0 - forward) * bwd_ref[pl.ds(hour, 1), :]
        angle = jnp.full((1, 2 * LANES), angle_ref[hour], F32)
        cosine = jnp.cos(angle)
        sine = jnp.sin(angle) * ((2.0 * forward - 1.0) / math.sqrt(LANES))
        kept = decay * cosine
        turned = decay * sine
        keep.append((kept[:, :LANES], kept[:, LANES:]))
        turn.append((-turned[:, :LANES], turned[:, LANES:]))
        decays.append((decay[:, :LANES], decay[:, LANES:]))
        angles += [cosine[:, :LANES], sine[:, :LANES]]
        table = (
            (site_ids == sites_ref[pl.ds(hour, 1), :]) & (slot_ids < count_ref[hour])
        ).astype(F32).astype(BF16)
        values = values_ref[hour]
        first = values.astype(BF16)
        rest = values - first.astype(F32)
        second = rest.astype(BF16)
        third = (rest - second.astype(F32)).astype(BF16)
        sums = dot(table, jnp.concatenate([first, second, third], axis=1))
        sums = sums[:, :LANES] + (sums[:, LANES : 2 * LANES] + sums[:, 2 * LANES :])
        sums = sums.T
        gain = gain_ref[pl.ds(hour, 1), :]
        source.append((sums * gain[:, :LANES], sums * gain[:, LANES:]))
        for h in range(2):
            source_ref[p, h] = source[p][h]

    for h in range(2):
        both = (
            keep[1][h] * source[0][h]
            + turn[1][h] * times_signs(source[0][1 - h], signs_twice)
            + source[1][h]
        )
        for s in range(2):
            for z in range(8):
                first_share = s * HALF + z * 8
                outbox[z, pl.ds(2 * h + s, 8, stride=4), :] = both[first_share : first_share + 8]
    quarter = lax.broadcasted_iota(jnp.int32, (1, LANES), 1) // 32
    packed = angles[0]
    for i in range(1, 4):
        packed = jnp.where(quarter == i, angles[i], packed)
    own_coefs[0:1, :] = packed
    for h in range(2):
        for p in range(2):
            own_coefs[pl.ds(1 + 2 * h + p, 1), :] = decays[p][h]

    pl.semaphore_wait(barrier, 15 + group)

    def slot(ref, k, part):
        return ref.at[pl.ds(k * TILE + part[0], part[1]), :]

    def to_peer(src, dst, peer, send, recv):
        return pltpu.make_async_remote_copy(
            src_ref=src,
            dst_ref=dst,
            send_sem=send,
            recv_sem=recv,
            device_id=peer,
            device_id_type=MESH,
        )

    five = pl.ds(0, COEFS[1])
    for z in line_mates:
        target = in_half(my_line, z)
        to_peer(
            own_coefs.at[five, :], line_coefs.at[my_z, five, :], target, send_sem.at[0], line_sem.at[0]
        ).start()
        to_peer(
            outbox.at[z], line_sources.at[my_z], target, send_sem.at[5], line_sem.at[1]
        ).start()
    line_coefs[my_z] = own_coefs[...]
    line_sources[my_z] = outbox[my_z]

    def bulk(ref, count, part, send, recv):
        rows = ref.at[pl.ds(0, count * part[1]), :]
        return to_peer(rows, rows, device(place), send, recv)

    def seven(ref, rows, send, recv):
        part = ref.at[pl.ds(0, 7), pl.ds(0, rows), :]
        return to_peer(part, part, device(place), send, recv)

    seven(line_coefs, COEFS[1], send_sem.at[0], line_sem.at[0]).wait_recv()
    seven(line_sources, 32, send_sem.at[5], line_sem.at[1]).wait_recv()

    blocks = pl.ds(my_line * 8, 8)
    for line in plane_mates:
        target = in_half(line, my_z)
        for src, part in (
            (line_coefs.at[:, five, :], COEFS),
            (line_sources.at[:, pl.ds(line * 4, 4), :], SOURCES),
        ):
            to_peer(
                src,
                inbox.at[blocks, pl.ds(*part), :],
                target,
                send_sem.at[6],
                inbox_sem.at[my_line],
            ).start()
    for z in range(8):
        inbox[my_line * 8 + z, pl.ds(*COEFS), :] = line_coefs[z, five, :]
        inbox[my_line * 8 + z, pl.ds(*SOURCES), :] = line_sources[z, pl.ds(my_line * 4, 4), :]

    def chunk_arrived(c):
        @pl.when(c != my_line)
        def _():
            part = inbox.at[pl.ds(0, 8), pl.ds(0, SOURCES[1] + COEFS[1]), :]
            to_peer(part, part, device(place), send_sem.at[6], inbox_sem.at[c]).wait_recv()

    tile_row = lax.broadcasted_iota(jnp.int32, (8, LANES), 0)
    tile_lane = lax.broadcasted_iota(jnp.int32, (8, LANES), 1)
    upper = ((tile_row == 2) & (tile_lane == share)) | (
        (tile_row == 3) & (tile_lane == share + HALF)
    )
    lower = ((tile_row == 4) & (tile_lane == share)) | (
        (tile_row == 5) & (tile_lane == share + HALF)
    )

    def coefficients(b):
        sources = inbox[b, pl.ds(0, 8), :]
        rows = inbox[b, pl.ds(8, 8), :]
        cosine, sine, next_cosine, next_sine = [
            jnp.broadcast_to(rows[0:1, 32 * i : 32 * i + 1], (1, LANES)) for i in range(4)
        ]
        decay = rows[1:2], rows[3:4]
        next_decay = rows[2:3], rows[4:5]
        return (
            [d * cosine for d in decay],
            [-decay[0] * sine, decay[1] * sine],
            [d * next_cosine for d in next_decay],
            [-next_decay[0] * next_sine, next_decay[1] * next_sine],
            sources,
        )

    def twice_turned(coefs):
        parts = []
        for turn_row in (coefs[1][1], coefs[1][0]):
            high, low = split(turn_row)
            left = jnp.concatenate(
                [signs_ref[:LANES, :] * high, signs_ref[:LANES, :] * low], axis=1
            )
            parts.append(split(dot(left, signs_ref[...])))
        (u_high, u_low), (l_high, l_low) = parts
        return jnp.concatenate(
            [
                jnp.concatenate([u_high, l_high], axis=1),
                jnp.concatenate([u_low, l_low], axis=1),
            ],
            axis=0,
        )

    def block(x, coefs, weights):
        keep_rows, turn_rows, next_keep, next_turn, sources = coefs
        high, low = split(x)
        kept = jnp.concatenate([keep_rows[0] * x[:8], keep_rows[1] * x[8:]], axis=0)
        turned = dot(
            jnp.concatenate(
                [
                    jnp.concatenate([high, low], axis=1),
                    jnp.concatenate(split(kept), axis=1),
                ],
                axis=0,
            ),
            signs_ref[...],
        )
        both = dot(
            jnp.concatenate(
                [
                    jnp.concatenate([high, high], axis=1),
                    jnp.concatenate([low, jnp.zeros_like(low)], axis=1),
                ],
                axis=0,
            ),
            weights,
        )
        source_u = jnp.where(tile_row >= 6, pltpu.roll(sources, 2, 0), 0.0)
        source_l = jnp.where(tile_row >= 6, sources, 0.0)
        u = (
            (next_keep[0] * kept[:8] + source_u)
            + (next_keep[0] * turn_rows[0]) * turned[8:16]
            + next_turn[0] * (turned[24:] + (both[:8, :LANES] + both[16:24, :LANES]))
        )
        l = (
            (next_keep[1] * kept[8:] + source_l)
            + (next_keep[1] * turn_rows[1]) * turned[:8]
            + next_turn[1] * (turned[16:24] + (both[8:16, LANES:] + both[24:, LANES:]))
        )
        return jnp.concatenate([u, l], axis=0)

    def keep_state(ref, at, x):
        ref[pl.ds(pl.multiple_of(at, TILE), 8), :] = x[:8]
        ref[pl.ds(at + 8, 2), :] = x[14:]
        ref[pl.ds(at + 10, 4), :] = x[10:14]

    def run(part):
        def run_chunk(c, carried):
            x, weights = carried

            @pl.when(c < HALF // CHUNK - 1)
            def _():
                chunk_arrived(c + 1)

            if part is STATE:
                @pl.when(c == HALF // CHUNK - 2)
                def _():
                    pl.semaphore_signal(
                        ready_sem, inc=1, device_id=device(me), device_id_type=MESH
                    )

            def send(b):
                own = (b == me).astype(jnp.int32)
                peer = b + own * (me + 1 - 2 * (me & 1) - b)
                to_peer(
                    slot(history, b, part),
                    slot(before, share + own * (HALF - share), part),
                    device(group * HALF + peer),
                    send_sem.at[1],
                    recv_sem.at[1],
                ).start()

            for k in range(CHUNK):
                b = c * CHUNK + k
                keep_state(history, b * TILE, x)
                following = twice_turned(coefficients(jnp.minimum(b + 1, HALF - 1)))
                x = block(x, coefficients(b), weights)
                weights = following
                if k % 2 == 1:
                    send(b - 1)
                    send(b)
            return x, weights

        chunk_arrived(0)
        x = jnp.concatenate([upper.astype(F32), lower.astype(F32)], axis=0)
        x, _ = lax.fori_loop(0, HALF // CHUNK, run_chunk, (x, twice_turned(coefficients(0))))
        keep_state(final, 0, x)

    @pl.when(group == 0)
    def _():
        run(SAMPLES)
        pl.semaphore_wait(ready_sem, 1)

        def conclude(k, carry):
            peer = ranked(k, k & 1)
            to_peer(
                slot(final, 0, SAMPLES),
                slot(ends, share, SAMPLES),
                device(HALF + peer),
                send_sem.at[2],
                recv_sem.at[2],
            ).start()
            return carry

        lax.fori_loop(0, HALF, conclude, 0)
        bulk(before, HALF, SAMPLES, send_sem.at[1], recv_sem.at[1]).wait_recv()

    @pl.when(group == 1)
    def _():
        run(STATE)
        bulk(before, HALF, STATE, send_sem.at[1], recv_sem.at[1]).wait_recv()

    before[pl.ds(pl.multiple_of(share * TILE, TILE), TILE), :] = history[
        pl.ds(pl.multiple_of(me * TILE, TILE), TILE), :
    ]

    def gathered(ref, at):
        return ref[pl.ds(at, HALF, stride=TILE), :]

    for h in range(2):
        for s in range(2):
            start_ref[h, pl.ds(s * HALF, HALF), :] = gathered(before, 6 + 2 * h + s)

    @pl.when(group == 1)
    def _():
        transfer = jnp.concatenate(
            [
                jnp.concatenate([gathered(before, 2 + 8 * h + i) for h in range(2)], axis=1)
                for i in range(4)
            ],
            axis=0,
        )
        transfer_high, transfer_low = split(transfer)
        bulk(ends, HALF, SAMPLES, send_sem.at[2], recv_sem.at[2]).wait_recv()
        entry = jnp.concatenate(
            [
                jnp.concatenate([gathered(ends, 6 + 2 * h + s) for h in range(2)], axis=1)
                for s in range(2)
            ],
            axis=0,
        )
        entry_high, entry_low = split(entry)
        moved = dot(jnp.concatenate([entry_high, entry_low], axis=0), transfer_high)
        moved = moved[:LANES] + (moved[LANES:] + dot(entry_high, transfer_low))
        for h in range(2):
            start_ref[h] += moved[:, h * LANES : (h + 1) * LANES]

    state = [start_ref[0], start_ref[1]]
    swaps = []
    for p in range(2):
        hour = p + row * (1 - 2 * p)
        turned = times_signs(jnp.concatenate(state, axis=0), signs_ref[...])
        bare = [
            keep[p][0] * state[0] + turn[p][0] * turned[LANES:],
            keep[p][1] * state[1] + turn[p][1] * turned[:LANES],
        ]
        state = [bare[h] + source_ref[p, h] for h in range(2)]
        mine_ref[0, hour] = jnp.where(row == 0, state[0], bare[1])
        mine_ref[1, hour] = jnp.where(row == 0, state[1], bare[0])
        swap = pltpu.make_async_remote_copy(
            src_ref=mine_ref.at[1, hour],
            dst_ref=theirs_ref.at[hour],
            send_sem=send_sem.at[3 + p],
            recv_sem=recv_sem.at[3 + hour],
            device_id=other_core,
            device_id_type=MESH,
        )
        swap.start()
        swaps.append(swap)

    for hour in range(2):
        pltpu.make_async_remote_copy(
            src_ref=theirs_ref.at[hour],
            dst_ref=theirs_ref.at[hour],
            send_sem=send_sem.at[3],
            recv_sem=recv_sem.at[3 + hour],
            device_id=other_core,
            device_id_type=MESH,
        ).wait_recv()
        own = mine_ref[0, hour]
        their = theirs_ref[hour]
        own_ref[hour] = own.T
        their_ref[hour] = their.T

    seven(line_coefs, COEFS[1], send_sem.at[0], line_sem.at[0]).wait_send()
    seven(line_sources, 32, send_sem.at[5], line_sem.at[1]).wait_send()
    passed = inbox.at[pl.ds(0, 7 * 8), pl.ds(0, SOURCES[1] + COEFS[1]), :]
    to_peer(passed, passed, device(place), send_sem.at[6], inbox_sem.at[0]).wait_send()

    @pl.when(group == 0)
    def _():
        bulk(history, HALF, SAMPLES, send_sem.at[1], recv_sem.at[1]).wait_send()
        bulk(ends, HALF, SAMPLES, send_sem.at[2], recv_sem.at[2]).wait_send()

    @pl.when(group == 1)
    def _():
        bulk(history, HALF, STATE, send_sem.at[1], recv_sem.at[1]).wait_send()

    for swap in swaps:
        swap.wait_send()


def local(decay_fwd, decay_bwd, angle, gain, obs_values, obs_sites, obs_count):
    args = (decay_fwd, decay_bwd, angle, gain, obs_values, obs_sites, obs_count)
    vmem = pl.BlockSpec(memory_space=pltpu.VMEM)
    out = jax.ShapeDtypeStruct((2, LANES, LANES), F32)
    box = pltpu.VMEM((HALF * TILE, LANES), F32)
    own, their = pl.pallas_call(
        kernel,
        out_shape=(out, out),
        in_specs=[pl.BlockSpec(memory_space=pl.ANY)] * len(args),
        out_specs=(vmem, vmem),
        scratch_shapes=[
            *(
                (pltpu.SMEM if arg.ndim == 1 else pltpu.VMEM)(arg.shape, arg.dtype)
                for arg in args
            ),
            pltpu.VMEM((8, 32, LANES), F32),
            pltpu.VMEM((8, LANES), F32),
            pltpu.VMEM((8, 32, LANES), F32),
            pltpu.VMEM((8, 8, LANES), F32),
            pltpu.VMEM((HALF, TILE, LANES), F32),
            box,
            pltpu.VMEM(((HALF + 1) * TILE, LANES), F32),
            pltpu.VMEM((TILE, LANES), F32),
            box,
            pltpu.VMEM((2 * LANES, LANES), BF16),
            pltpu.VMEM((2, 2, LANES, LANES), F32),
            pltpu.VMEM((2, LANES, LANES), F32),
            pltpu.VMEM((2, 2, LANES, LANES), F32),
            pltpu.VMEM((2, LANES, LANES), F32),
            pltpu.SemaphoreType.DMA((len(args),)),
            pltpu.SemaphoreType.DMA((7,)),
            pltpu.SemaphoreType.DMA((5,)),
            pltpu.SemaphoreType.DMA((2,)),
            pltpu.SemaphoreType.DMA((HALF // CHUNK,)),
            pltpu.SemaphoreType.REGULAR,
        ],
        compiler_params=pltpu.CompilerParams(
            collective_id=1, has_side_effects=True, vmem_limit_bytes=32 * 2**20
        ),
        name="smoother",
    )(*(pltpu.with_memory_space_constraint(arg, pltpu.HBM) for arg in args))
    return jnp.where(lax.axis_index("row") == 0, own, their), own + their


def solution(mesh):
    return jax.shard_map(
        local,
        mesh=mesh,
        in_specs=(
            P("tm", None),
            P("tm", None),
            P("tm"),
            P("tm", None),
            P("tm", None, None),
            P("tm", None),
            P("tm"),
        ),
        out_specs=(P("tm", "row", None), P("tm", "row", None)),
        check_vma=False,
    )
```

```python
import math

import jax
import jax.numpy as jnp
from jax import lax
from jax.experimental import pallas as pl
from jax.experimental.pallas import tpu as pltpu
from jax.sharding import PartitionSpec as P

MESH = pl.DeviceIdType.MESH
F32 = jnp.float32
BF16 = jnp.bfloat16
HALF = 64
CHUNK = 8
TILE = 16
LANES = 128
STATE = (2, 12)
SAMPLES = (6, 4)
SOURCES = (4, 4)
COEFS = (8, 5)


def split(x):
    high = x.astype(BF16)
    low = (x - high.astype(F32)).astype(BF16)
    return high, low


def dot(x, y):
    return jnp.dot(x, y, preferred_element_type=F32)


def times_signs(x, signs_twice):
    return dot(jnp.concatenate(split(x), axis=1), signs_twice)


def sign_matrix():
    shared = lax.broadcasted_iota(jnp.int32, (LANES, LANES), 0) & lax.broadcasted_iota(
        jnp.int32, (LANES, LANES), 1
    )
    for shift in (4, 2, 1):
        shared = shared ^ (shared >> shift)
    return (1 - 2 * (shared & 1)).astype(F32).astype(BF16)


def kernel(
    fwd_hbm,
    bwd_hbm,
    angle_hbm,
    gain_hbm,
    values_hbm,
    sites_hbm,
    count_hbm,
    own_ref,
    their_ref,
    fwd_ref,
    bwd_ref,
    angle_ref,
    gain_ref,
    values_ref,
    sites_ref,
    count_ref,
    outbox,
    own_coefs,
    line_sources,
    plane_coefs,
    inbox,
    history,
    before,
    final,
    ends,
    signs_ref,
    source_ref,
    moves_ref,
    mine_ref,
    theirs_ref,
    load_sem,
    send_sem,
    recv_sem,
    line_sem,
    inbox_sem,
    ready_sem,
):
    loads = [
        pltpu.make_async_copy(src, dst, load_sem.at[i])
        for i, (src, dst) in enumerate(
            (
                (values_hbm, values_ref),
                (sites_hbm, sites_ref),
                (count_hbm, count_ref),
                (fwd_hbm, fwd_ref),
                (bwd_hbm, bwd_ref),
                (gain_hbm, gain_ref),
                (angle_hbm, angle_ref),
            )
        )
    ]
    for load in loads:
        load.start()

    row = lax.axis_index("row")
    tm = lax.axis_index("tm")
    place = tm + row * (2 * HALF - 1 - 2 * tm)
    group = place >> 6
    me = place & 63
    my_x, my_y, my_z, my_line = me >> 5, (me >> 3) & 3, me & 7, me >> 3
    share = my_z * 8 + my_line

    def device(a_place):
        return (a_place + row * (2 * HALF - 1 - 2 * a_place), row)

    other_core = (tm, 1 - row)

    def ranked(k, x_step):
        by_z, by_y = k >> 3, (k >> 1) & 3
        z = my_z + 4 + ((by_z + 1) >> 1) * (2 * (by_z & 1) - 1)
        y = my_y + 2 + ((by_y + 1) >> 1) * (2 * (by_y & 1) - 1)
        x = my_x + x_step
        return ((x & 1) << 5) + ((y & 3) << 3) + (z & 7)

    line_mates = [(my_z + step) & 7 for step in (4, 5, 3, 6, 2, 7, 1)]
    plane_mates = [
        (((my_x + x_step) & 1) << 2) + ((my_y + y_step) & 3)
        for x_step, y_step in ((1, 2), (1, 1), (1, 3), (0, 2), (1, 0), (0, 1), (0, 3))
    ]

    def in_half(line, z):
        return device(group * HALF + line * 8 + z)

    barrier = pltpu.get_barrier_semaphore()

    def greet(target):
        pl.semaphore_signal(barrier, inc=1, device_id=target, device_id_type=MESH)

    for z in line_mates:
        greet(in_half(my_line, z))
    for line in plane_mates:
        greet(in_half(line, my_z))
    greet(other_core)

    @pl.when(group == 0)
    def _():
        greet(device(HALF + me))

    signs = sign_matrix()
    signs_twice = jnp.concatenate([signs, signs], axis=0)
    signs_ref[...] = signs_twice
    slot_ids = lax.broadcasted_iota(jnp.int32, (LANES, 64), 1)
    site_ids = lax.broadcasted_iota(jnp.int32, (LANES, 64), 0)
    forward = (row == 0).astype(F32)
    for load in loads:
        load.wait()
    keep, turn, source, decays, angles = [], [], [], [], []
    for p in range(2):
        hour = p + row * (1 - 2 * p)
        decay = forward * fwd_ref[pl.ds(hour, 1), :] + (1.0 - forward) * bwd_ref[pl.ds(hour, 1), :]
        angle = jnp.full((1, 2 * LANES), angle_ref[hour], F32)
        cosine = jnp.cos(angle)
        sine = jnp.sin(angle) * ((2.0 * forward - 1.0) / math.sqrt(LANES))
        kept = decay * cosine
        turned = decay * sine
        keep.append((kept[:, :LANES], kept[:, LANES:]))
        turn.append((-turned[:, :LANES], turned[:, LANES:]))
        decays.append((decay[:, :LANES], decay[:, LANES:]))
        angles += [cosine[:, :LANES], sine[:, :LANES]]
        table = (
            (site_ids == sites_ref[pl.ds(hour, 1), :]) & (slot_ids < count_ref[hour])
        ).astype(F32).astype(BF16)
        values = values_ref[hour]
        first = values.astype(BF16)
        rest = values - first.astype(F32)
        second = rest.astype(BF16)
        third = (rest - second.astype(F32)).astype(BF16)
        sums = dot(table, jnp.concatenate([first, second, third], axis=1))
        sums = sums[:, :LANES] + (sums[:, LANES : 2 * LANES] + sums[:, 2 * LANES :])
        sums = sums.T
        gain = gain_ref[pl.ds(hour, 1), :]
        source.append((sums * gain[:, :LANES], sums * gain[:, LANES:]))
        for h in range(2):
            source_ref[p, h] = source[p][h]

    for h in range(2):
        both = (
            keep[1][h] * source[0][h]
            + turn[1][h] * times_signs(source[0][1 - h], signs_twice)
            + source[1][h]
        )
        for s in range(2):
            for z in range(8):
                first_share = s * HALF + z * 8
                outbox[z, pl.ds(2 * h + s, 8, stride=4), :] = both[first_share : first_share + 8]
    quarter = lax.broadcasted_iota(jnp.int32, (1, LANES), 1) // 32
    packed = angles[0]
    for i in range(1, 4):
        packed = jnp.where(quarter == i, angles[i], packed)
    own_coefs[0:1, :] = packed
    for h in range(2):
        for p in range(2):
            own_coefs[pl.ds(1 + 2 * h + p, 1), :] = decays[p][h]

    pl.semaphore_wait(barrier, 15 + group)

    def slot(ref, k, part):
        return ref.at[pl.ds(k * TILE + part[0], part[1]), :]

    def to_peer(src, dst, peer, send, recv):
        return pltpu.make_async_remote_copy(
            src_ref=src,
            dst_ref=dst,
            send_sem=send,
            recv_sem=recv,
            device_id=peer,
            device_id_type=MESH,
        )

    five = pl.ds(0, COEFS[1])
    for line in plane_mates:
        to_peer(
            own_coefs.at[five, :],
            plane_coefs.at[my_line, five, :],
            in_half(line, my_z),
            send_sem.at[0],
            line_sem.at[0],
        ).start()
    for part, x in enumerate((1 - my_x, my_x)):
        rows = pl.ds(16 * x, 16)
        for z in line_mates:
            to_peer(
                outbox.at[z, rows, :],
                line_sources.at[my_z, rows, :],
                in_half(my_line, z),
                send_sem.at[5],
                line_sem.at[1 + part],
            ).start()
    plane_coefs[my_line] = own_coefs[...]
    line_sources[my_z] = outbox[my_z]

    def bulk(ref, count, part, send, recv):
        rows = ref.at[pl.ds(0, count * part[1]), :]
        return to_peer(rows, rows, device(place), send, recv)

    def seven(ref, rows, send, recv):
        part = ref.at[pl.ds(0, 7), pl.ds(0, rows), :]
        return to_peer(part, part, device(place), send, recv)

    seven(plane_coefs, COEFS[1], send_sem.at[0], line_sem.at[0]).wait_recv()
    def pass_coefs(part):
        lines = pl.ds(4 * part, 4)
        for z in line_mates:
            to_peer(
                plane_coefs.at[lines, five, :],
                inbox.at[lines, my_z, pl.ds(*COEFS), :],
                in_half(my_line, z),
                send_sem.at[7],
                line_sem.at[3 + part],
            ).start()

    pass_coefs(0)
    for part, x in enumerate((1 - my_x, my_x)):
        seven(line_sources, 16, send_sem.at[5], line_sem.at[1 + part]).wait_recv()
        for y_step in (2, 1, 3, 0)[: 4 - part]:
            line = x * 4 + ((my_y + y_step) & 3)
            to_peer(
                line_sources.at[:, pl.ds(line * 4, 4), :],
                inbox.at[my_line, :, pl.ds(*SOURCES), :],
                in_half(line, my_z),
                send_sem.at[6],
                inbox_sem.at[my_line],
            ).start()
    pass_coefs(1)
    for k in range(8):
        inbox[k, my_z, pl.ds(*COEFS), :] = plane_coefs[k, five, :]
        inbox[my_line, k, pl.ds(*SOURCES), :] = line_sources[k, pl.ds(my_line * 4, 4), :]

    def second_leg(part, send, recv):
        rows = inbox.at[pl.ds(0, 7), :, pl.ds(0, part[1]), :]
        return to_peer(rows, rows, device(place), send, recv)

    def coefs_arrived(part):
        rows = inbox.at[pl.ds(0, 4), pl.ds(0, 7), pl.ds(0, COEFS[1]), :]
        to_peer(rows, rows, device(place), send_sem.at[7], line_sem.at[3 + part]).wait_recv()

    coefs_arrived(0)

    def chunk_arrived(c):
        @pl.when(c != my_line)
        def _():
            rows = inbox.at[0, :, pl.ds(0, SOURCES[1]), :]
            to_peer(rows, rows, device(place), send_sem.at[6], inbox_sem.at[c]).wait_recv()

    tile_row = lax.broadcasted_iota(jnp.int32, (8, LANES), 0)
    tile_lane = lax.broadcasted_iota(jnp.int32, (8, LANES), 1)
    upper = ((tile_row == 2) & (tile_lane == share)) | (
        (tile_row == 3) & (tile_lane == share + HALF)
    )
    lower = ((tile_row == 4) & (tile_lane == share)) | (
        (tile_row == 5) & (tile_lane == share + HALF)
    )

    def coefficients(b):
        sources = inbox[b >> 3, b & 7, pl.ds(0, 8), :]
        rows = inbox[b >> 3, b & 7, pl.ds(8, 8), :]
        cosine, sine, next_cosine, next_sine = [
            jnp.broadcast_to(rows[0:1, 32 * i : 32 * i + 1], (1, LANES)) for i in range(4)
        ]
        decay = rows[1:2], rows[3:4]
        next_decay = rows[2:3], rows[4:5]
        return (
            [d * cosine for d in decay],
            [-decay[0] * sine, decay[1] * sine],
            [d * next_cosine for d in next_decay],
            [-next_decay[0] * next_sine, next_decay[1] * next_sine],
            sources,
        )

    def twice_turned(coefs):
        parts = []
        for turn_row in (coefs[1][1], coefs[1][0]):
            high, low = split(turn_row)
            left = jnp.concatenate(
                [signs_ref[:LANES, :] * high, signs_ref[:LANES, :] * low], axis=1
            )
            parts.append(split(dot(left, signs_ref[...])))
        (u_high, u_low), (l_high, l_low) = parts
        return jnp.concatenate(
            [
                jnp.concatenate([u_high, l_high], axis=1),
                jnp.concatenate([u_low, l_low], axis=1),
            ],
            axis=0,
        )

    def block(x, coefs, weights):
        keep_rows, turn_rows, next_keep, next_turn, sources = coefs
        high, low = split(x)
        kept = jnp.concatenate([keep_rows[0] * x[:8], keep_rows[1] * x[8:]], axis=0)
        turned = dot(
            jnp.concatenate(
                [
                    jnp.concatenate([high, low], axis=1),
                    jnp.concatenate(split(kept), axis=1),
                ],
                axis=0,
            ),
            signs_ref[...],
        )
        both = dot(
            jnp.concatenate(
                [
                    jnp.concatenate([high, high], axis=1),
                    jnp.concatenate([low, jnp.zeros_like(low)], axis=1),
                ],
                axis=0,
            ),
            weights,
        )
        source_u = jnp.where(tile_row >= 6, pltpu.roll(sources, 2, 0), 0.0)
        source_l = jnp.where(tile_row >= 6, sources, 0.0)
        u = (
            (next_keep[0] * kept[:8] + source_u)
            + (next_keep[0] * turn_rows[0]) * turned[8:16]
            + next_turn[0] * (turned[24:] + (both[:8, :LANES] + both[16:24, :LANES]))
        )
        l = (
            (next_keep[1] * kept[8:] + source_l)
            + (next_keep[1] * turn_rows[1]) * turned[:8]
            + next_turn[1] * (turned[16:24] + (both[8:16, LANES:] + both[24:, LANES:]))
        )
        return jnp.concatenate([u, l], axis=0)

    def keep_state(ref, at, x):
        ref[pl.ds(pl.multiple_of(at, TILE), 8), :] = x[:8]
        ref[pl.ds(at + 8, 2), :] = x[14:]
        ref[pl.ds(at + 10, 4), :] = x[10:14]

    def run(part):
        def run_chunk(c, carried):
            x, weights = carried

            @pl.when(c < HALF // CHUNK - 1)
            def _():
                chunk_arrived(c + 1)

            @pl.when(c == 3)
            def _():
                coefs_arrived(1)

            if part is STATE:
                @pl.when(c == HALF // CHUNK - 2)
                def _():
                    pl.semaphore_signal(
                        ready_sem, inc=1, device_id=device(me), device_id_type=MESH
                    )

            def send(b):
                own = (b == me).astype(jnp.int32)
                peer = b + own * (me + 1 - 2 * (me & 1) - b)
                to_peer(
                    slot(history, b, part),
                    slot(before, share + own * (HALF - share), part),
                    device(group * HALF + peer),
                    send_sem.at[1],
                    recv_sem.at[1],
                ).start()

            for k in range(CHUNK):
                b = c * CHUNK + k
                keep_state(history, b * TILE, x)
                following = twice_turned(coefficients(jnp.minimum(b + 1, HALF - 1)))
                x = block(x, coefficients(b), weights)
                weights = following
                if k % 2 == 1:
                    send(b - 1)
                    send(b)
            return x, weights

        chunk_arrived(0)
        x = jnp.concatenate([upper.astype(F32), lower.astype(F32)], axis=0)
        x, _ = lax.fori_loop(0, HALF // CHUNK, run_chunk, (x, twice_turned(coefficients(0))))
        keep_state(final, 0, x)

    @pl.when(group == 0)
    def _():
        run(SAMPLES)
        pl.semaphore_wait(ready_sem, 1)

        def conclude(k, carry):
            peer = ranked(k, k & 1)
            to_peer(
                slot(final, 0, SAMPLES),
                slot(ends, share, SAMPLES),
                device(HALF + peer),
                send_sem.at[2],
                recv_sem.at[2],
            ).start()
            return carry

        lax.fori_loop(0, HALF, conclude, 0)
        bulk(before, HALF, SAMPLES, send_sem.at[1], recv_sem.at[1]).wait_recv()

    @pl.when(group == 1)
    def _():
        run(STATE)
        bulk(before, HALF, STATE, send_sem.at[1], recv_sem.at[1]).wait_recv()

    before[pl.ds(pl.multiple_of(share * TILE, TILE), TILE), :] = history[
        pl.ds(pl.multiple_of(me * TILE, TILE), TILE), :
    ]

    def gathered(ref, at):
        return ref[pl.ds(at, HALF, stride=TILE), :]

    def hour_of(p):
        return p + row * (1 - 2 * p)

    def swap(p):
        hour = hour_of(p)
        return to_peer(
            mine_ref.at[1, hour],
            theirs_ref.at[hour],
            other_core,
            send_sem.at[3 + p],
            recv_sem.at[3 + hour],
        )

    def own_hours(with_transfer):
        halves = [
            jnp.concatenate([gathered(before, 6 + 2 * h + s) for s in range(2)], axis=0)
            for h in range(2)
        ]
        if with_transfer:
            halves = [
                jnp.concatenate(
                    [halves[h]] + [gathered(before, 2 + 8 * h + i) for i in range(4)], axis=0
                )
                for h in range(2)
            ]
        count = halves[0].shape[0]
        for p in range(2):
            turned = times_signs(jnp.concatenate(halves, axis=0), signs_ref[...])
            halves = [
                keep[p][0] * halves[0] + turn[p][0] * turned[count:],
                keep[p][1] * halves[1] + turn[p][1] * turned[:count],
            ]
            bare = [half[:LANES] for half in halves]
            full = [bare[h] + source_ref[p, h] for h in range(2)]
            mine_ref[0, hour_of(p)] = jnp.where(row == 0, full[0], bare[1])
            mine_ref[1, hour_of(p)] = jnp.where(row == 0, full[1], bare[0])
            if with_transfer:
                columns = [half[LANES:] for half in halves]
                for q in range(2):
                    chosen = jnp.where(row == 0, columns[q], columns[1 - q])
                    moves_ref[p, q, 0], moves_ref[p, q, 1] = split(chosen)
                full = [jnp.concatenate([full[h], columns[h]], axis=0) for h in range(2)]
            else:
                swap(p).start()
            halves = full

    @pl.when(group == 0)
    def _():
        own_hours(False)

    @pl.when(group == 1)
    def _():
        own_hours(True)
        bulk(ends, HALF, SAMPLES, send_sem.at[2], recv_sem.at[2]).wait_recv()
        entry = jnp.concatenate(
            [
                jnp.concatenate([gathered(ends, 6 + 2 * h + s) for h in range(2)], axis=1)
                for s in range(2)
            ],
            axis=0,
        )
        entry_high, entry_low = split(entry)
        entry_both = jnp.concatenate([entry_high, entry_low], axis=0)
        for q in (1, 0):
            for p in range(2):
                moved = dot(entry_both, moves_ref[p, q, 0])
                mine_ref[q, hour_of(p)] += moved[:LANES] + (
                    moved[LANES:] + dot(entry_high, moves_ref[p, q, 1])
                )
                if q == 1:
                    swap(p).start()

    for hour in range(2):
        pltpu.make_async_remote_copy(
            src_ref=theirs_ref.at[hour],
            dst_ref=theirs_ref.at[hour],
            send_sem=send_sem.at[3],
            recv_sem=recv_sem.at[3 + hour],
            device_id=other_core,
            device_id_type=MESH,
        ).wait_recv()
        own = mine_ref[0, hour]
        their = theirs_ref[hour]
        own_ref[hour] = own.T
        their_ref[hour] = their.T

    seven(plane_coefs, COEFS[1], send_sem.at[0], line_sem.at[0]).wait_send()
    seven(line_sources, 32, send_sem.at[5], line_sem.at[1]).wait_send()
    second_leg(SOURCES, send_sem.at[6], line_sem.at[0]).wait_send()
    second_leg(COEFS, send_sem.at[7], line_sem.at[0]).wait_send()

    @pl.when(group == 0)
    def _():
        bulk(history, HALF, SAMPLES, send_sem.at[1], recv_sem.at[1]).wait_send()
        bulk(ends, HALF, SAMPLES, send_sem.at[2], recv_sem.at[2]).wait_send()

    @pl.when(group == 1)
    def _():
        bulk(history, HALF, STATE, send_sem.at[1], recv_sem.at[1]).wait_send()

    for p in range(2):
        swap(p).wait_send()


def local(decay_fwd, decay_bwd, angle, gain, obs_values, obs_sites, obs_count):
    args = (decay_fwd, decay_bwd, angle, gain, obs_values, obs_sites, obs_count)
    vmem = pl.BlockSpec(memory_space=pltpu.VMEM)
    out = jax.ShapeDtypeStruct((2, LANES, LANES), F32)
    box = pltpu.VMEM((HALF * TILE, LANES), F32)
    own, their = pl.pallas_call(
        kernel,
        out_shape=(out, out),
        in_specs=[pl.BlockSpec(memory_space=pl.ANY)] * len(args),
        out_specs=(vmem, vmem),
        scratch_shapes=[
            *(
                (pltpu.SMEM if arg.ndim == 1 else pltpu.VMEM)(arg.shape, arg.dtype)
                for arg in args
            ),
            pltpu.VMEM((8, 32, LANES), F32),
            pltpu.VMEM((8, LANES), F32),
            pltpu.VMEM((8, 32, LANES), F32),
            pltpu.VMEM((8, 8, LANES), F32),
            pltpu.VMEM((8, 8, TILE, LANES), F32),
            box,
            pltpu.VMEM(((HALF + 1) * TILE, LANES), F32),
            pltpu.VMEM((TILE, LANES), F32),
            box,
            pltpu.VMEM((2 * LANES, LANES), BF16),
            pltpu.VMEM((2, 2, LANES, LANES), F32),
            pltpu.VMEM((2, 2, 2, 2 * LANES, LANES), BF16),
            pltpu.VMEM((2, 2, LANES, LANES), F32),
            pltpu.VMEM((2, LANES, LANES), F32),
            pltpu.SemaphoreType.DMA((len(args),)),
            pltpu.SemaphoreType.DMA((8,)),
            pltpu.SemaphoreType.DMA((5,)),
            pltpu.SemaphoreType.DMA((5,)),
            pltpu.SemaphoreType.DMA((HALF // CHUNK,)),
            pltpu.SemaphoreType.REGULAR,
        ],
        compiler_params=pltpu.CompilerParams(
            collective_id=1, has_side_effects=True, vmem_limit_bytes=32 * 2**20
        ),
        name="smoother",
    )(*(pltpu.with_memory_space_constraint(arg, pltpu.HBM) for arg in args))
    return jnp.where(lax.axis_index("row") == 0, own, their), own + their


def solution(mesh):
    return jax.shard_map(
        local,
        mesh=mesh,
        in_specs=(
            P("tm", None),
            P("tm", None),
            P("tm"),
            P("tm", None),
            P("tm", None, None),
            P("tm", None),
            P("tm"),
        ),
        out_specs=(P("tm", "row", None), P("tm", "row", None)),
        check_vma=False,
    )
```

```python
import math

import jax
import jax.numpy as jnp
from jax import lax
from jax.experimental import pallas as pl
from jax.experimental.pallas import tpu as pltpu
from jax.sharding import PartitionSpec as P

MESH = pl.DeviceIdType.MESH
F32 = jnp.float32
BF16 = jnp.bfloat16
HALF = 64
STEPS = 16
TILE = 16
LANES = 128
STATE = (2, 12)
SAMPLES = (6, 4)
SOURCES = (4, 4)
COEFS = (8, 5)


def split(x):
    high = x.astype(BF16)
    low = (x - high.astype(F32)).astype(BF16)
    return high, low


def dot(x, y):
    return jnp.dot(x, y, preferred_element_type=F32)


def times_signs(x, signs_twice):
    return dot(jnp.concatenate(split(x), axis=1), signs_twice)


def sign_matrix():
    shared = lax.broadcasted_iota(jnp.int32, (LANES, LANES), 0) & lax.broadcasted_iota(
        jnp.int32, (LANES, LANES), 1
    )
    for shift in (4, 2, 1):
        shared = shared ^ (shared >> shift)
    return (1 - 2 * (shared & 1)).astype(F32).astype(BF16)


def kernel(
    fwd_hbm,
    bwd_hbm,
    angle_hbm,
    gain_hbm,
    values_hbm,
    sites_hbm,
    count_hbm,
    own_ref,
    their_ref,
    fwd_ref,
    bwd_ref,
    angle_ref,
    gain_ref,
    values_ref,
    sites_ref,
    count_ref,
    outbox,
    own_coefs,
    line_sources,
    plane_coefs,
    inbox,
    history,
    before,
    final,
    ends,
    signs_ref,
    source_ref,
    moves_ref,
    mine_ref,
    theirs_ref,
    load_sem,
    send_sem,
    recv_sem,
    line_sem,
    inbox_sem,
    ready_sem,
):
    loads = [
        pltpu.make_async_copy(src, dst, load_sem.at[i])
        for i, (src, dst) in enumerate(
            (
                (values_hbm, values_ref),
                (sites_hbm, sites_ref),
                (count_hbm, count_ref),
                (fwd_hbm, fwd_ref),
                (bwd_hbm, bwd_ref),
                (gain_hbm, gain_ref),
                (angle_hbm, angle_ref),
            )
        )
    ]
    row = lax.axis_index("row")
    tm = lax.axis_index("tm")
    place = tm + row * (2 * HALF - 1 - 2 * tm)
    group = place >> 6
    me = place & 63
    my_x, my_y, my_z, my_line = me >> 5, (me >> 3) & 3, me & 7, me >> 3
    share = my_z * 8 + my_line

    def device(a_place):
        return (a_place + row * (2 * HALF - 1 - 2 * a_place), row)

    other_core = (tm, 1 - row)

    def ranked(k, x_step):
        by_z, by_y = k >> 3, (k >> 1) & 3
        z = my_z + 4 + ((by_z + 1) >> 1) * (2 * (by_z & 1) - 1)
        y = my_y + 2 + ((by_y + 1) >> 1) * (2 * (by_y & 1) - 1)
        x = my_x + x_step
        return ((x & 1) << 5) + ((y & 3) << 3) + (z & 7)

    line_mates = [(my_z + step) & 7 for step in (4, 5, 3, 6, 2, 7, 1)]
    plane_mates = [
        (((my_x + x_step) & 1) << 2) + ((my_y + y_step) & 3)
        for x_step, y_step in ((1, 2), (1, 1), (1, 3), (0, 2), (1, 0), (0, 1), (0, 3))
    ]

    def in_half(line, z):
        return device(group * HALF + line * 8 + z)

    barrier = pltpu.get_barrier_semaphore()

    def greet(target):
        pl.semaphore_signal(barrier, inc=1, device_id=target, device_id_type=MESH)

    for z in line_mates:
        greet(in_half(my_line, z))
    for line in plane_mates:
        greet(in_half(line, my_z))
    greet(other_core)

    @pl.when(group == 0)
    def _():
        greet(device(HALF + me))

    for load in loads:
        load.start()

    signs = sign_matrix()
    signs_twice = jnp.concatenate([signs, signs], axis=0)
    signs_ref[...] = signs_twice
    slot_ids = lax.broadcasted_iota(jnp.int32, (LANES, 64), 1)
    site_ids = lax.broadcasted_iota(jnp.int32, (LANES, 64), 0)
    forward = (row == 0).astype(F32)
    for load in loads:
        load.wait()
    keep, turn, source, decays, angles = [], [], [], [], []
    for p in range(2):
        hour = p + row * (1 - 2 * p)
        decay = forward * fwd_ref[pl.ds(hour, 1), :] + (1.0 - forward) * bwd_ref[pl.ds(hour, 1), :]
        angle = jnp.full((1, 2 * LANES), angle_ref[hour], F32)
        cosine = jnp.cos(angle)
        sine = jnp.sin(angle) * ((2.0 * forward - 1.0) / math.sqrt(LANES))
        kept = decay * cosine
        turned = decay * sine
        keep.append((kept[:, :LANES], kept[:, LANES:]))
        turn.append((-turned[:, :LANES], turned[:, LANES:]))
        decays.append((decay[:, :LANES], decay[:, LANES:]))
        angles += [cosine[:, :LANES], sine[:, :LANES]]
        table = (
            (site_ids == sites_ref[pl.ds(hour, 1), :]) & (slot_ids < count_ref[hour])
        ).astype(F32).astype(BF16)
        values = values_ref[hour]
        first = values.astype(BF16)
        rest = values - first.astype(F32)
        second = rest.astype(BF16)
        third = (rest - second.astype(F32)).astype(BF16)
        sums = dot(table, jnp.concatenate([first, second, third], axis=1))
        sums = sums[:, :LANES] + (sums[:, LANES : 2 * LANES] + sums[:, 2 * LANES :])
        sums = sums.T
        gain = gain_ref[pl.ds(hour, 1), :]
        source.append((sums * gain[:, :LANES], sums * gain[:, LANES:]))
        for h in range(2):
            source_ref[p, h] = source[p][h]

    for h in range(2):
        both = (
            keep[1][h] * source[0][h]
            + turn[1][h] * times_signs(source[0][1 - h], signs_twice)
            + source[1][h]
        )
        for s in range(2):
            for z in range(8):
                first_share = s * HALF + z * 8
                outbox[z, pl.ds(2 * h + s, 8, stride=4), :] = both[first_share : first_share + 8]
    quarter = lax.broadcasted_iota(jnp.int32, (1, LANES), 1) // 32
    packed = angles[0]
    for i in range(1, 4):
        packed = jnp.where(quarter == i, angles[i], packed)
    own_coefs[0:1, :] = packed
    for h in range(2):
        for p in range(2):
            own_coefs[pl.ds(1 + 2 * h + p, 1), :] = decays[p][h]

    pl.semaphore_wait(barrier, 15 + group)

    def slot(ref, k, part):
        return ref.at[pl.ds(k * TILE + part[0], part[1]), :]

    def to_peer(src, dst, peer, send, recv):
        return pltpu.make_async_remote_copy(
            src_ref=src,
            dst_ref=dst,
            send_sem=send,
            recv_sem=recv,
            device_id=peer,
            device_id_type=MESH,
        )

    five = pl.ds(0, COEFS[1])
    def share_sources(part, x):
        rows = pl.ds(16 * x, 16)
        for z in line_mates:
            to_peer(
                outbox.at[z, rows, :],
                line_sources.at[my_z, rows, :],
                in_half(my_line, z),
                send_sem.at[5],
                line_sem.at[1 + part],
            ).start()

    share_sources(0, 1 - my_x)
    for line in plane_mates:
        to_peer(
            own_coefs.at[five, :],
            plane_coefs.at[my_line, five, :],
            in_half(line, my_z),
            send_sem.at[0],
            line_sem.at[0],
        ).start()
    share_sources(1, my_x)
    plane_coefs[my_line] = own_coefs[...]
    line_sources[my_z] = outbox[my_z]

    def bulk(ref, count, part, send, recv):
        rows = ref.at[pl.ds(0, count * part[1]), :]
        return to_peer(rows, rows, device(place), send, recv)

    def seven(ref, rows, send, recv):
        part = ref.at[pl.ds(0, 7), pl.ds(0, rows), :]
        return to_peer(part, part, device(place), send, recv)

    seven(plane_coefs, COEFS[1], send_sem.at[0], line_sem.at[0]).wait_recv()
    def pass_coefs(part):
        lines = pl.ds(4 * part, 4)
        for z in line_mates:
            to_peer(
                plane_coefs.at[lines, five, :],
                inbox.at[lines, my_z, pl.ds(*COEFS), :],
                in_half(my_line, z),
                send_sem.at[7],
                line_sem.at[3 + part],
            ).start()

    pass_coefs(0)
    for part, x in enumerate((1 - my_x, my_x)):
        seven(line_sources, 16, send_sem.at[5], line_sem.at[1 + part]).wait_recv()
        for y_step in (2, 1, 3, 0)[: 4 - part]:
            line = x * 4 + ((my_y + y_step) & 3)
            to_peer(
                line_sources.at[:, pl.ds(line * 4, 4), :],
                inbox.at[my_line, :, pl.ds(*SOURCES), :],
                in_half(line, my_z),
                send_sem.at[6],
                inbox_sem.at[my_line],
            ).start()
    pass_coefs(1)
    for k in range(8):
        inbox[k, my_z, pl.ds(*COEFS), :] = plane_coefs[k, five, :]
        inbox[my_line, k, pl.ds(*SOURCES), :] = line_sources[k, pl.ds(my_line * 4, 4), :]

    def second_leg(part, send, recv):
        rows = inbox.at[pl.ds(0, 7), :, pl.ds(0, part[1]), :]
        return to_peer(rows, rows, device(place), send, recv)

    def coefs_arrived(part):
        rows = inbox.at[pl.ds(0, 4), pl.ds(0, 7), pl.ds(0, COEFS[1]), :]
        to_peer(rows, rows, device(place), send_sem.at[7], line_sem.at[3 + part]).wait_recv()

    coefs_arrived(0)

    def chunk_arrived(c):
        @pl.when(c != my_line)
        def _():
            rows = inbox.at[0, :, pl.ds(0, SOURCES[1]), :]
            to_peer(rows, rows, device(place), send_sem.at[6], inbox_sem.at[c]).wait_recv()

    tile_row = lax.broadcasted_iota(jnp.int32, (8, LANES), 0)
    tile_lane = lax.broadcasted_iota(jnp.int32, (8, LANES), 1)
    upper = ((tile_row == 2) & (tile_lane == share)) | (
        (tile_row == 3) & (tile_lane == share + HALF)
    )
    lower = ((tile_row == 4) & (tile_lane == share)) | (
        (tile_row == 5) & (tile_lane == share + HALF)
    )

    def coefficients(b):
        sources = inbox[b >> 3, b & 7, pl.ds(0, 8), :]
        rows = inbox[b >> 3, b & 7, pl.ds(8, 8), :]
        cosine, sine, next_cosine, next_sine = [
            jnp.broadcast_to(rows[0:1, 32 * i : 32 * i + 1], (1, LANES)) for i in range(4)
        ]
        decay = rows[1:2], rows[3:4]
        next_decay = rows[2:3], rows[4:5]
        return (
            [d * cosine for d in decay],
            [-decay[0] * sine, decay[1] * sine],
            [d * next_cosine for d in next_decay],
            [-next_decay[0] * next_sine, next_decay[1] * next_sine],
            sources,
        )

    def twice_turned(coefs):
        parts = []
        for turn_row in (coefs[1][1], coefs[1][0]):
            high, low = split(turn_row)
            left = jnp.concatenate(
                [signs_ref[:LANES, :] * high, signs_ref[:LANES, :] * low], axis=1
            )
            parts.append(split(dot(left, signs_ref[...])))
        (u_high, u_low), (l_high, l_low) = parts
        return jnp.concatenate(
            [
                jnp.concatenate([u_high, l_high], axis=1),
                jnp.concatenate([u_low, l_low], axis=1),
            ],
            axis=0,
        )

    def block(x, coefs, weights):
        keep_rows, turn_rows, next_keep, next_turn, sources = coefs
        high, low = split(x)
        kept = jnp.concatenate([keep_rows[0] * x[:8], keep_rows[1] * x[8:]], axis=0)
        turned = dot(
            jnp.concatenate(
                [
                    jnp.concatenate([high, low], axis=1),
                    jnp.concatenate(split(kept), axis=1),
                ],
                axis=0,
            ),
            signs_ref[...],
        )
        both = dot(
            jnp.concatenate(
                [
                    jnp.concatenate([high, high], axis=1),
                    jnp.concatenate([low, jnp.zeros_like(low)], axis=1),
                ],
                axis=0,
            ),
            weights,
        )
        source_u = jnp.where(tile_row >= 6, pltpu.roll(sources, 2, 0), 0.0)
        source_l = jnp.where(tile_row >= 6, sources, 0.0)
        u = (
            (next_keep[0] * kept[:8] + source_u)
            + (next_keep[0] * turn_rows[0]) * turned[8:16]
            + next_turn[0] * (turned[24:] + (both[:8, :LANES] + both[16:24, :LANES]))
        )
        l = (
            (next_keep[1] * kept[8:] + source_l)
            + (next_keep[1] * turn_rows[1]) * turned[:8]
            + next_turn[1] * (turned[16:24] + (both[8:16, LANES:] + both[24:, LANES:]))
        )
        return jnp.concatenate([u, l], axis=0)

    def keep_state(ref, at, x):
        ref[pl.ds(pl.multiple_of(at, TILE), 8), :] = x[:8]
        ref[pl.ds(at + 8, 2), :] = x[14:]
        ref[pl.ds(at + 10, 4), :] = x[10:14]

    def run(part):
        def run_chunk(c, carried):
            x, weights = carried

            for i in range(STEPS // 8):
                chunk_arrived(c * (STEPS // 8) + i)

            @pl.when(c == HALF // STEPS // 2 - 1)
            def _():
                coefs_arrived(1)

            if part is STATE:
                @pl.when(c == HALF // STEPS - 1)
                def _():
                    pl.semaphore_signal(
                        ready_sem, inc=1, device_id=device(me), device_id_type=MESH
                    )

            def send(b):
                own = (b == me).astype(jnp.int32)
                peer = b + own * (me + 1 - 2 * (me & 1) - b)
                to_peer(
                    slot(history, b, part),
                    slot(before, share + own * (HALF - share), part),
                    device(group * HALF + peer),
                    send_sem.at[1],
                    recv_sem.at[1],
                ).start()

            for k in range(STEPS):
                b = c * STEPS + k
                keep_state(history, b * TILE, x)
                following = twice_turned(coefficients(jnp.minimum(b + 1, HALF - 1)))
                x = block(x, coefficients(b), weights)
                weights = following
                if k % 2 == 1:
                    send(b - 1)
                    send(b)
            return x, weights

        x = jnp.concatenate([upper.astype(F32), lower.astype(F32)], axis=0)
        x, _ = lax.fori_loop(0, HALF // STEPS, run_chunk, (x, twice_turned(coefficients(0))))
        keep_state(final, 0, x)

    @pl.when(group == 0)
    def _():
        run(SAMPLES)
        pl.semaphore_wait(ready_sem, 1)

        def conclude(k, carry):
            peer = ranked(k, k & 1)
            to_peer(
                slot(final, 0, SAMPLES),
                slot(ends, share, SAMPLES),
                device(HALF + peer),
                send_sem.at[2],
                recv_sem.at[2],
            ).start()
            return carry

        lax.fori_loop(0, HALF, conclude, 0)
        bulk(before, HALF, SAMPLES, send_sem.at[1], recv_sem.at[1]).wait_recv()

    @pl.when(group == 1)
    def _():
        run(STATE)
        bulk(before, HALF, STATE, send_sem.at[1], recv_sem.at[1]).wait_recv()

    before[pl.ds(pl.multiple_of(share * TILE, TILE), TILE), :] = history[
        pl.ds(pl.multiple_of(me * TILE, TILE), TILE), :
    ]

    def gathered(ref, at):
        return ref[pl.ds(at, HALF, stride=TILE), :]

    def hour_of(p):
        return p + row * (1 - 2 * p)

    def swap(p):
        hour = hour_of(p)
        return to_peer(
            mine_ref.at[1, hour],
            theirs_ref.at[hour],
            other_core,
            send_sem.at[3 + p],
            recv_sem.at[3 + hour],
        )

    def own_hours(with_transfer):
        halves = [
            jnp.concatenate([gathered(before, 6 + 2 * h + s) for s in range(2)], axis=0)
            for h in range(2)
        ]
        if with_transfer:
            halves = [
                jnp.concatenate(
                    [halves[h]] + [gathered(before, 2 + 8 * h + i) for i in range(4)], axis=0
                )
                for h in range(2)
            ]
        count = halves[0].shape[0]
        for p in range(2):
            turned = times_signs(jnp.concatenate(halves, axis=0), signs_ref[...])
            halves = [
                keep[p][0] * halves[0] + turn[p][0] * turned[count:],
                keep[p][1] * halves[1] + turn[p][1] * turned[:count],
            ]
            bare = [half[:LANES] for half in halves]
            full = [bare[h] + source_ref[p, h] for h in range(2)]
            mine_ref[0, hour_of(p)] = jnp.where(row == 0, full[0], bare[1])
            mine_ref[1, hour_of(p)] = jnp.where(row == 0, full[1], bare[0])
            if with_transfer:
                columns = [half[LANES:] for half in halves]
                for q in range(2):
                    chosen = jnp.where(row == 0, columns[q], columns[1 - q])
                    moves_ref[p, q, 0], moves_ref[p, q, 1] = split(chosen)
                full = [jnp.concatenate([full[h], columns[h]], axis=0) for h in range(2)]
            else:
                swap(p).start()
            halves = full

    @pl.when(group == 0)
    def _():
        own_hours(False)

    @pl.when(group == 1)
    def _():
        own_hours(True)
        bulk(ends, HALF, SAMPLES, send_sem.at[2], recv_sem.at[2]).wait_recv()
        entry = jnp.concatenate(
            [
                jnp.concatenate([gathered(ends, 6 + 2 * h + s) for h in range(2)], axis=1)
                for s in range(2)
            ],
            axis=0,
        )
        entry_high, entry_low = split(entry)
        entry_both = jnp.concatenate([entry_high, entry_low], axis=0)
        for q in (1, 0):
            for p in range(2):
                moved = dot(entry_both, moves_ref[p, q, 0])
                mine_ref[q, hour_of(p)] += moved[:LANES] + (
                    moved[LANES:] + dot(entry_high, moves_ref[p, q, 1])
                )
                if q == 1:
                    swap(p).start()

    for hour in range(2):
        pltpu.make_async_remote_copy(
            src_ref=theirs_ref.at[hour],
            dst_ref=theirs_ref.at[hour],
            send_sem=send_sem.at[3],
            recv_sem=recv_sem.at[3 + hour],
            device_id=other_core,
            device_id_type=MESH,
        ).wait_recv()
        own = mine_ref[0, hour]
        their = theirs_ref[hour]
        own_ref[hour] = own.T
        their_ref[hour] = their.T

    seven(plane_coefs, COEFS[1], send_sem.at[0], line_sem.at[0]).wait_send()
    seven(line_sources, 32, send_sem.at[5], line_sem.at[1]).wait_send()
    second_leg(SOURCES, send_sem.at[6], line_sem.at[0]).wait_send()
    second_leg(COEFS, send_sem.at[7], line_sem.at[0]).wait_send()

    @pl.when(group == 0)
    def _():
        bulk(history, HALF, SAMPLES, send_sem.at[1], recv_sem.at[1]).wait_send()
        bulk(ends, HALF, SAMPLES, send_sem.at[2], recv_sem.at[2]).wait_send()

    @pl.when(group == 1)
    def _():
        bulk(history, HALF, STATE, send_sem.at[1], recv_sem.at[1]).wait_send()

    for p in range(2):
        swap(p).wait_send()


def local(decay_fwd, decay_bwd, angle, gain, obs_values, obs_sites, obs_count):
    args = (decay_fwd, decay_bwd, angle, gain, obs_values, obs_sites, obs_count)
    vmem = pl.BlockSpec(memory_space=pltpu.VMEM)
    out = jax.ShapeDtypeStruct((2, LANES, LANES), F32)
    box = pltpu.VMEM((HALF * TILE, LANES), F32)
    own, their = pl.pallas_call(
        kernel,
        out_shape=(out, out),
        in_specs=[pl.BlockSpec(memory_space=pl.ANY)] * len(args),
        out_specs=(vmem, vmem),
        scratch_shapes=[
            *(
                (pltpu.SMEM if arg.ndim == 1 else pltpu.VMEM)(arg.shape, arg.dtype)
                for arg in args
            ),
            pltpu.VMEM((8, 32, LANES), F32),
            pltpu.VMEM((8, LANES), F32),
            pltpu.VMEM((8, 32, LANES), F32),
            pltpu.VMEM((8, 8, LANES), F32),
            pltpu.VMEM((8, 8, TILE, LANES), F32),
            box,
            pltpu.VMEM(((HALF + 1) * TILE, LANES), F32),
            pltpu.VMEM((TILE, LANES), F32),
            box,
            pltpu.VMEM((2 * LANES, LANES), BF16),
            pltpu.VMEM((2, 2, LANES, LANES), F32),
            pltpu.VMEM((2, 2, 2, 2 * LANES, LANES), BF16),
            pltpu.VMEM((2, 2, LANES, LANES), F32),
            pltpu.VMEM((2, LANES, LANES), F32),
            pltpu.SemaphoreType.DMA((len(args),)),
            pltpu.SemaphoreType.DMA((8,)),
            pltpu.SemaphoreType.DMA((5,)),
            pltpu.SemaphoreType.DMA((5,)),
            pltpu.SemaphoreType.DMA((8,)),
            pltpu.SemaphoreType.REGULAR,
        ],
        compiler_params=pltpu.CompilerParams(
            collective_id=1, has_side_effects=True, vmem_limit_bytes=32 * 2**20
        ),
        name="smoother",
    )(*(pltpu.with_memory_space_constraint(arg, pltpu.HBM) for arg in args))
    return jnp.where(lax.axis_index("row") == 0, own, their), own + their


def solution(mesh):
    return jax.shard_map(
        local,
        mesh=mesh,
        in_specs=(
            P("tm", None),
            P("tm", None),
            P("tm"),
            P("tm", None),
            P("tm", None, None),
            P("tm", None),
            P("tm"),
        ),
        out_specs=(P("tm", "row", None), P("tm", "row", None)),
        check_vma=False,
    )
```

```python
import math

import jax
import jax.numpy as jnp
from jax import lax
from jax.experimental import pallas as pl
from jax.experimental.pallas import tpu as pltpu
from jax.sharding import PartitionSpec as P

MESH = pl.DeviceIdType.MESH
F32 = jnp.float32
BF16 = jnp.bfloat16
HALF = 64
STEPS = 16
TILE = 16
LANES = 128
STATE = (2, 12)
SAMPLES = (6, 4)
SOURCES = (4, 4)
COEFS = (8, 5)


def split(x):
    high = x.astype(BF16)
    low = (x - high.astype(F32)).astype(BF16)
    return high, low


def dot(x, y):
    return jnp.dot(x, y, preferred_element_type=F32)


def times_signs(x, signs_twice):
    return dot(jnp.concatenate(split(x), axis=1), signs_twice)


def sign_matrix():
    shared = lax.broadcasted_iota(jnp.int32, (LANES, LANES), 0) & lax.broadcasted_iota(
        jnp.int32, (LANES, LANES), 1
    )
    for shift in (4, 2, 1):
        shared = shared ^ (shared >> shift)
    return (1 - 2 * (shared & 1)).astype(F32).astype(BF16)


def kernel(
    fwd_hbm,
    bwd_hbm,
    angle_hbm,
    gain_hbm,
    values_hbm,
    sites_hbm,
    count_hbm,
    own_ref,
    their_ref,
    fwd_ref,
    bwd_ref,
    angle_ref,
    gain_ref,
    values_ref,
    sites_ref,
    count_ref,
    outbox,
    own_coefs,
    line_sources,
    plane_coefs,
    inbox,
    history,
    before,
    final,
    ends,
    signs_ref,
    source_ref,
    moves_ref,
    mine_ref,
    theirs_ref,
    load_sem,
    send_sem,
    recv_sem,
    line_sem,
    inbox_sem,
    ready_sem,
):
    loads = [
        pltpu.make_async_copy(src, dst, load_sem.at[i])
        for i, (src, dst) in enumerate(
            (
                (values_hbm, values_ref),
                (sites_hbm, sites_ref),
                (count_hbm, count_ref),
                (fwd_hbm, fwd_ref),
                (bwd_hbm, bwd_ref),
                (gain_hbm, gain_ref),
                (angle_hbm, angle_ref),
            )
        )
    ]
    row = lax.axis_index("row")
    tm = lax.axis_index("tm")
    place = tm + row * (2 * HALF - 1 - 2 * tm)
    group = place >> 6
    me = place & 63
    my_x, my_y, my_z, my_line = me >> 5, (me >> 3) & 3, me & 7, me >> 3
    share = my_z * 8 + my_line

    def device(a_place):
        return (a_place + row * (2 * HALF - 1 - 2 * a_place), row)

    other_core = (tm, 1 - row)

    def ranked(k, x_step):
        by_z, by_y = k >> 3, (k >> 1) & 3
        z = my_z + 4 + ((by_z + 1) >> 1) * (2 * (by_z & 1) - 1)
        y = my_y + 2 + ((by_y + 1) >> 1) * (2 * (by_y & 1) - 1)
        x = my_x + x_step
        return ((x & 1) << 5) + ((y & 3) << 3) + (z & 7)

    line_mates = [(my_z + step) & 7 for step in (4, 5, 3, 6, 2, 7, 1)]
    plane_mates = [
        (((my_x + x_step) & 1) << 2) + ((my_y + y_step) & 3)
        for x_step, y_step in ((1, 2), (1, 1), (1, 3), (0, 2), (1, 0), (0, 1), (0, 3))
    ]

    def in_half(line, z):
        return device(group * HALF + line * 8 + z)

    barrier = pltpu.get_barrier_semaphore()

    def greet(target):
        pl.semaphore_signal(barrier, inc=1, device_id=target, device_id_type=MESH)

    for z in line_mates:
        greet(in_half(my_line, z))
    for line in plane_mates:
        greet(in_half(line, my_z))
    greet(other_core)

    @pl.when(group == 0)
    def _():
        greet(device(HALF + me))

    for load in loads:
        load.start()

    signs = sign_matrix()
    signs_twice = jnp.concatenate([signs, signs], axis=0)
    signs_ref[...] = signs_twice
    slot_ids = lax.broadcasted_iota(jnp.int32, (LANES, 64), 1)
    site_ids = lax.broadcasted_iota(jnp.int32, (LANES, 64), 0)
    forward = (row == 0).astype(F32)
    for load in loads:
        load.wait()
    keep, turn, source, decays, angles = [], [], [], [], []
    for p in range(2):
        hour = p + row * (1 - 2 * p)
        decay = forward * fwd_ref[pl.ds(hour, 1), :] + (1.0 - forward) * bwd_ref[pl.ds(hour, 1), :]
        angle = jnp.full((1, 2 * LANES), angle_ref[hour], F32)
        cosine = jnp.cos(angle)
        sine = jnp.sin(angle) * ((2.0 * forward - 1.0) / math.sqrt(LANES))
        kept = decay * cosine
        turned = decay * sine
        keep.append((kept[:, :LANES], kept[:, LANES:]))
        turn.append((-turned[:, :LANES], turned[:, LANES:]))
        decays.append((decay[:, :LANES], decay[:, LANES:]))
        angles += [cosine[:, :LANES], sine[:, :LANES]]
        table = (
            (site_ids == sites_ref[pl.ds(hour, 1), :]) & (slot_ids < count_ref[hour])
        ).astype(F32).astype(BF16)
        values = values_ref[hour]
        first = values.astype(BF16)
        rest = values - first.astype(F32)
        second = rest.astype(BF16)
        third = (rest - second.astype(F32)).astype(BF16)
        sums = dot(table, jnp.concatenate([first, second, third], axis=1))
        sums = sums[:, :LANES] + (sums[:, LANES : 2 * LANES] + sums[:, 2 * LANES :])
        sums = sums.T
        gain = gain_ref[pl.ds(hour, 1), :]
        source.append((sums * gain[:, :LANES], sums * gain[:, LANES:]))
        for h in range(2):
            source_ref[p, h] = source[p][h]

    for h in range(2):
        both = (
            keep[1][h] * source[0][h]
            + turn[1][h] * times_signs(source[0][1 - h], signs_twice)
            + source[1][h]
        )
        for s in range(2):
            for z in range(8):
                first_share = s * HALF + z * 8
                outbox[z, pl.ds(2 * h + s, 8, stride=4), :] = both[first_share : first_share + 8]
    quarter = lax.broadcasted_iota(jnp.int32, (1, LANES), 1) // 32
    packed = angles[0]
    for i in range(1, 4):
        packed = jnp.where(quarter == i, angles[i], packed)
    own_coefs[0:1, :] = packed
    for h in range(2):
        for p in range(2):
            own_coefs[pl.ds(1 + 2 * h + p, 1), :] = decays[p][h]

    pl.semaphore_wait(barrier, 15 + group)

    def slot(ref, k, part):
        return ref.at[pl.ds(k * TILE + part[0], part[1]), :]

    def to_peer(src, dst, peer, send, recv):
        return pltpu.make_async_remote_copy(
            src_ref=src,
            dst_ref=dst,
            send_sem=send,
            recv_sem=recv,
            device_id=peer,
            device_id_type=MESH,
        )

    five = pl.ds(0, COEFS[1])
    def share_sources(part, x):
        rows = pl.ds(16 * x, 16)
        for z in line_mates:
            to_peer(
                outbox.at[z, rows, :],
                line_sources.at[my_z, rows, :],
                in_half(my_line, z),
                send_sem.at[5],
                line_sem.at[1 + part],
            ).start()

    share_sources(0, 1 - my_x)
    for line in plane_mates:
        to_peer(
            own_coefs.at[five, :],
            plane_coefs.at[my_line, five, :],
            in_half(line, my_z),
            send_sem.at[0],
            line_sem.at[0],
        ).start()
    share_sources(1, my_x)
    plane_coefs[my_line] = own_coefs[...]
    line_sources[my_z] = outbox[my_z]

    def bulk(ref, count, part, send, recv):
        rows = ref.at[pl.ds(0, count * part[1]), :]
        return to_peer(rows, rows, device(place), send, recv)

    def seven(ref, rows, send, recv):
        part = ref.at[pl.ds(0, 7), pl.ds(0, rows), :]
        return to_peer(part, part, device(place), send, recv)

    seven(plane_coefs, COEFS[1], send_sem.at[0], line_sem.at[0]).wait_recv()
    def pass_coefs(part):
        lines = pl.ds(4 * part, 4)
        for z in line_mates:
            to_peer(
                plane_coefs.at[lines, five, :],
                inbox.at[lines, my_z, pl.ds(*COEFS), :],
                in_half(my_line, z),
                send_sem.at[7],
                line_sem.at[3 + part],
            ).start()

    pass_coefs(0)
    pass_coefs(1)
    for part, x in enumerate((1 - my_x, my_x)):
        seven(line_sources, 16, send_sem.at[5], line_sem.at[1 + part]).wait_recv()
        for y_step in (2, 1, 3, 0)[: 4 - part]:
            line = x * 4 + ((my_y + y_step) & 3)
            to_peer(
                line_sources.at[:, pl.ds(line * 4, 4), :],
                inbox.at[my_line, :, pl.ds(*SOURCES), :],
                in_half(line, my_z),
                send_sem.at[6],
                inbox_sem.at[my_line],
            ).start()
    pltpu.make_async_copy(
        line_sources.at[:, pl.ds(my_line * 4, 4), :],
        inbox.at[my_line, :, pl.ds(*SOURCES), :],
        inbox_sem.at[my_line],
    ).start()
    for k in range(8):
        inbox[k, my_z, pl.ds(*COEFS), :] = plane_coefs[k, five, :]

    def second_leg(part, send, recv):
        rows = inbox.at[pl.ds(0, 7), :, pl.ds(0, part[1]), :]
        return to_peer(rows, rows, device(place), send, recv)

    def coefs_arrived(part):
        rows = inbox.at[pl.ds(0, 4), pl.ds(0, 7), pl.ds(0, COEFS[1]), :]
        to_peer(rows, rows, device(place), send_sem.at[7], line_sem.at[3 + part]).wait_recv()

    coefs_arrived(0)

    def chunk_arrived(c):
        rows = inbox.at[0, :, pl.ds(0, SOURCES[1]), :]
        pltpu.make_async_copy(rows, rows, inbox_sem.at[c]).wait()

    tile_row = lax.broadcasted_iota(jnp.int32, (8, LANES), 0)
    tile_lane = lax.broadcasted_iota(jnp.int32, (8, LANES), 1)
    upper = ((tile_row == 2) & (tile_lane == share)) | (
        (tile_row == 3) & (tile_lane == share + HALF)
    )
    lower = ((tile_row == 4) & (tile_lane == share)) | (
        (tile_row == 5) & (tile_lane == share + HALF)
    )

    def coefficients(b):
        sources = inbox[b >> 3, b & 7, pl.ds(0, 8), :]
        rows = inbox[b >> 3, b & 7, pl.ds(8, 8), :]
        cosine, sine, next_cosine, next_sine = [
            jnp.broadcast_to(rows[0:1, 32 * i : 32 * i + 1], (1, LANES)) for i in range(4)
        ]
        decay = rows[1:2], rows[3:4]
        next_decay = rows[2:3], rows[4:5]
        return (
            [d * cosine for d in decay],
            [-decay[0] * sine, decay[1] * sine],
            [d * next_cosine for d in next_decay],
            [-next_decay[0] * next_sine, next_decay[1] * next_sine],
            sources,
        )

    def twice_turned(coefs):
        parts = []
        for turn_row in (coefs[1][1], coefs[1][0]):
            high, low = split(turn_row)
            left = jnp.concatenate(
                [signs_ref[:LANES, :] * high, signs_ref[:LANES, :] * low], axis=1
            )
            parts.append(split(dot(left, signs_ref[...])))
        (u_high, u_low), (l_high, l_low) = parts
        return jnp.concatenate(
            [
                jnp.concatenate([u_high, l_high], axis=1),
                jnp.concatenate([u_low, l_low], axis=1),
            ],
            axis=0,
        )

    def block(x, coefs, weights):
        keep_rows, turn_rows, next_keep, next_turn, sources = coefs
        high, low = split(x)
        kept = jnp.concatenate([keep_rows[0] * x[:8], keep_rows[1] * x[8:]], axis=0)
        turned = dot(
            jnp.concatenate(
                [
                    jnp.concatenate([high, low], axis=1),
                    jnp.concatenate(split(kept), axis=1),
                ],
                axis=0,
            ),
            signs_ref[...],
        )
        both = dot(
            jnp.concatenate(
                [
                    jnp.concatenate([high, high], axis=1),
                    jnp.concatenate([low, jnp.zeros_like(low)], axis=1),
                ],
                axis=0,
            ),
            weights,
        )
        source_u = jnp.where(tile_row >= 6, pltpu.roll(sources, 2, 0), 0.0)
        source_l = jnp.where(tile_row >= 6, sources, 0.0)
        u = (
            (next_keep[0] * kept[:8] + source_u)
            + (next_keep[0] * turn_rows[0]) * turned[8:16]
            + next_turn[0] * (turned[24:] + (both[:8, :LANES] + both[16:24, :LANES]))
        )
        l = (
            (next_keep[1] * kept[8:] + source_l)
            + (next_keep[1] * turn_rows[1]) * turned[:8]
            + next_turn[1] * (turned[16:24] + (both[8:16, LANES:] + both[24:, LANES:]))
        )
        return jnp.concatenate([u, l], axis=0)

    def keep_state(ref, at, x):
        ref[pl.ds(pl.multiple_of(at, TILE), 8), :] = x[:8]
        ref[pl.ds(at + 8, 2), :] = x[14:]
        ref[pl.ds(at + 10, 4), :] = x[10:14]

    def run(part):
        def run_chunk(c, carried):
            x, weights = carried

            for i in range(STEPS // 8):
                chunk_arrived(c * (STEPS // 8) + i)

            @pl.when(c == HALF // STEPS // 2 - 1)
            def _():
                coefs_arrived(1)

            if part is STATE:
                @pl.when(c == HALF // STEPS - 1)
                def _():
                    pl.semaphore_signal(
                        ready_sem, inc=1, device_id=device(me), device_id_type=MESH
                    )

            def send(b):
                own = (b == me).astype(jnp.int32)
                peer = b + own * (me + 1 - 2 * (me & 1) - b)
                to_peer(
                    slot(history, b, part),
                    slot(before, share + own * (HALF - share), part),
                    device(group * HALF + peer),
                    send_sem.at[1],
                    recv_sem.at[1],
                ).start()

            for k in range(STEPS):
                b = c * STEPS + k
                keep_state(history, b * TILE, x)
                following = twice_turned(coefficients(jnp.minimum(b + 1, HALF - 1)))
                x = block(x, coefficients(b), weights)
                weights = following
                if k % 2 == 1:
                    send(b - 1)
                    send(b)
            return x, weights

        x = jnp.concatenate([upper.astype(F32), lower.astype(F32)], axis=0)
        x, _ = lax.fori_loop(0, HALF // STEPS, run_chunk, (x, twice_turned(coefficients(0))))
        keep_state(final, 0, x)

    @pl.when(group == 0)
    def _():
        run(SAMPLES)
        pl.semaphore_wait(ready_sem, 1)

        def conclude(k, carry):
            peer = ranked(k, k & 1)
            to_peer(
                slot(final, 0, SAMPLES),
                slot(ends, share, SAMPLES),
                device(HALF + peer),
                send_sem.at[2],
                recv_sem.at[2],
            ).start()
            return carry

        lax.fori_loop(0, HALF, conclude, 0, unroll=8)
        bulk(before, HALF, SAMPLES, send_sem.at[1], recv_sem.at[1]).wait_recv()

    @pl.when(group == 1)
    def _():
        run(STATE)
        bulk(before, HALF, STATE, send_sem.at[1], recv_sem.at[1]).wait_recv()

    before[pl.ds(pl.multiple_of(share * TILE, TILE), TILE), :] = history[
        pl.ds(pl.multiple_of(me * TILE, TILE), TILE), :
    ]

    def gathered(ref, at):
        return ref[pl.ds(at, HALF, stride=TILE), :]

    def hour_of(p):
        return p + row * (1 - 2 * p)

    def swap(p):
        hour = hour_of(p)
        return to_peer(
            mine_ref.at[1, hour],
            theirs_ref.at[hour],
            other_core,
            send_sem.at[3 + p],
            recv_sem.at[3 + hour],
        )

    def own_hours(with_transfer):
        halves = [
            jnp.concatenate([gathered(before, 6 + 2 * h + s) for s in range(2)], axis=0)
            for h in range(2)
        ]
        if with_transfer:
            halves = [
                jnp.concatenate(
                    [halves[h]] + [gathered(before, 2 + 8 * h + i) for i in range(4)], axis=0
                )
                for h in range(2)
            ]
        count = halves[0].shape[0]
        for p in range(2):
            turned = times_signs(jnp.concatenate(halves, axis=0), signs_ref[...])
            halves = [
                keep[p][0] * halves[0] + turn[p][0] * turned[count:],
                keep[p][1] * halves[1] + turn[p][1] * turned[:count],
            ]
            bare = [half[:LANES] for half in halves]
            full = [bare[h] + source_ref[p, h] for h in range(2)]
            mine_ref[0, hour_of(p)] = jnp.where(row == 0, full[0], bare[1])
            mine_ref[1, hour_of(p)] = jnp.where(row == 0, full[1], bare[0])
            if with_transfer:
                columns = [half[LANES:] for half in halves]
                for q in range(2):
                    chosen = jnp.where(row == 0, columns[q], columns[1 - q])
                    moves_ref[p, q, 0], moves_ref[p, q, 1] = split(chosen)
                full = [jnp.concatenate([full[h], columns[h]], axis=0) for h in range(2)]
            else:
                swap(p).start()
            halves = full

    @pl.when(group == 0)
    def _():
        own_hours(False)

    @pl.when(group == 1)
    def _():
        own_hours(True)
        bulk(ends, HALF, SAMPLES, send_sem.at[2], recv_sem.at[2]).wait_recv()
        entry = jnp.concatenate(
            [
                jnp.concatenate([gathered(ends, 6 + 2 * h + s) for h in range(2)], axis=1)
                for s in range(2)
            ],
            axis=0,
        )
        entry_high, entry_low = split(entry)
        entry_both = jnp.concatenate([entry_high, entry_low], axis=0)
        for q in (1, 0):
            for p in range(2):
                moved = dot(entry_both, moves_ref[p, q, 0])
                mine_ref[q, hour_of(p)] += moved[:LANES] + (
                    moved[LANES:] + dot(entry_high, moves_ref[p, q, 1])
                )
                if q == 1:
                    swap(p).start()

    for hour in range(2):
        own_ref[hour] = mine_ref[0, hour].T
    for p in range(2):
        hour = hour_of(1 - p)
        to_peer(
            theirs_ref.at[hour],
            theirs_ref.at[hour],
            other_core,
            send_sem.at[3],
            recv_sem.at[3 + hour],
        ).wait_recv()
        their_ref[hour] = theirs_ref[hour].T

    seven(plane_coefs, COEFS[1], send_sem.at[0], line_sem.at[0]).wait_send()
    seven(line_sources, 32, send_sem.at[5], line_sem.at[1]).wait_send()
    second_leg(SOURCES, send_sem.at[6], line_sem.at[0]).wait_send()
    second_leg(COEFS, send_sem.at[7], line_sem.at[0]).wait_send()

    @pl.when(group == 0)
    def _():
        bulk(history, HALF, SAMPLES, send_sem.at[1], recv_sem.at[1]).wait_send()
        bulk(ends, HALF, SAMPLES, send_sem.at[2], recv_sem.at[2]).wait_send()

    @pl.when(group == 1)
    def _():
        bulk(history, HALF, STATE, send_sem.at[1], recv_sem.at[1]).wait_send()

    for p in range(2):
        swap(p).wait_send()


def local(decay_fwd, decay_bwd, angle, gain, obs_values, obs_sites, obs_count):
    args = (decay_fwd, decay_bwd, angle, gain, obs_values, obs_sites, obs_count)
    vmem = pl.BlockSpec(memory_space=pltpu.VMEM)
    out = jax.ShapeDtypeStruct((2, LANES, LANES), F32)
    box = pltpu.VMEM((HALF * TILE, LANES), F32)
    own, their = pl.pallas_call(
        kernel,
        out_shape=(out, out),
        in_specs=[pl.BlockSpec(memory_space=pl.ANY)] * len(args),
        out_specs=(vmem, vmem),
        scratch_shapes=[
            *(
                (pltpu.SMEM if arg.ndim == 1 else pltpu.VMEM)(arg.shape, arg.dtype)
                for arg in args
            ),
            pltpu.VMEM((8, 32, LANES), F32),
            pltpu.VMEM((8, LANES), F32),
            pltpu.VMEM((8, 32, LANES), F32),
            pltpu.VMEM((8, 8, LANES), F32),
            pltpu.VMEM((8, 8, TILE, LANES), F32),
            box,
            pltpu.VMEM(((HALF + 1) * TILE, LANES), F32),
            pltpu.VMEM((TILE, LANES), F32),
            box,
            pltpu.VMEM((2 * LANES, LANES), BF16),
            pltpu.VMEM((2, 2, LANES, LANES), F32),
            pltpu.VMEM((2, 2, 2, 2 * LANES, LANES), BF16),
            pltpu.VMEM((2, 2, LANES, LANES), F32),
            pltpu.VMEM((2, LANES, LANES), F32),
            pltpu.SemaphoreType.DMA((len(args),)),
            pltpu.SemaphoreType.DMA((8,)),
            pltpu.SemaphoreType.DMA((5,)),
            pltpu.SemaphoreType.DMA((5,)),
            pltpu.SemaphoreType.DMA((8,)),
            pltpu.SemaphoreType.REGULAR,
        ],
        compiler_params=pltpu.CompilerParams(
            collective_id=1, has_side_effects=True, vmem_limit_bytes=32 * 2**20
        ),
        name="smoother",
    )(*(pltpu.with_memory_space_constraint(arg, pltpu.HBM) for arg in args))
    return jnp.where(lax.axis_index("row") == 0, own, their), own + their


def solution(mesh):
    return jax.shard_map(
        local,
        mesh=mesh,
        in_specs=(
            P("tm", None),
            P("tm", None),
            P("tm"),
            P("tm", None),
            P("tm", None, None),
            P("tm", None),
            P("tm"),
        ),
        out_specs=(P("tm", "row", None), P("tm", "row", None)),
        check_vma=False,
    )
```

```python
import math

import jax
import jax.numpy as jnp
from jax import lax
from jax.experimental import pallas as pl
from jax.experimental.pallas import tpu as pltpu
from jax.sharding import PartitionSpec as P

MESH = pl.DeviceIdType.MESH
F32 = jnp.float32
BF16 = jnp.bfloat16
HALF = 64
STEPS = 16
TILE = 16
LANES = 128
STATE = (2, 12)
SAMPLES = (6, 4)
SOURCES = (4, 4)
COEFS = (8, 5)


def split(x):
    high = x.astype(BF16)
    low = (x - high.astype(F32)).astype(BF16)
    return high, low


def dot(x, y):
    return jnp.dot(x, y, preferred_element_type=F32)


def times_signs(x, signs_twice):
    return dot(jnp.concatenate(split(x), axis=1), signs_twice)


def sign_matrix():
    shared = lax.broadcasted_iota(jnp.int32, (LANES, LANES), 0) & lax.broadcasted_iota(
        jnp.int32, (LANES, LANES), 1
    )
    for shift in (4, 2, 1):
        shared = shared ^ (shared >> shift)
    return (1 - 2 * (shared & 1)).astype(F32).astype(BF16)


def kernel(
    fwd_hbm,
    bwd_hbm,
    angle_hbm,
    gain_hbm,
    values_hbm,
    sites_hbm,
    count_hbm,
    own_ref,
    their_ref,
    fwd_ref,
    bwd_ref,
    angle_ref,
    gain_ref,
    values_ref,
    sites_ref,
    count_ref,
    outbox,
    own_coefs,
    line_sources,
    plane_coefs,
    inbox,
    history,
    before,
    final,
    ends,
    signs_ref,
    source_ref,
    moves_ref,
    mine_ref,
    theirs_ref,
    load_sem,
    send_sem,
    recv_sem,
    line_sem,
    inbox_sem,
    ready_sem,
):
    loads = [
        pltpu.make_async_copy(src, dst, load_sem.at[i])
        for i, (src, dst) in enumerate(
            (
                (values_hbm, values_ref),
                (sites_hbm, sites_ref),
                (count_hbm, count_ref),
                (fwd_hbm, fwd_ref),
                (bwd_hbm, bwd_ref),
                (gain_hbm, gain_ref),
                (angle_hbm, angle_ref),
            )
        )
    ]
    row = lax.axis_index("row")
    tm = lax.axis_index("tm")
    place = tm + row * (2 * HALF - 1 - 2 * tm)
    group = place >> 6
    me = place & 63
    my_x, my_y, my_z, my_line = me >> 5, (me >> 3) & 3, me & 7, me >> 3
    share = my_z * 8 + my_line

    def device(a_place):
        return (a_place + row * (2 * HALF - 1 - 2 * a_place), row)

    other_core = (tm, 1 - row)

    def ranked(k, x_step):
        by_z, by_y = k >> 3, (k >> 1) & 3
        z = my_z + 4 + ((by_z + 1) >> 1) * (2 * (by_z & 1) - 1)
        y = my_y + 2 + ((by_y + 1) >> 1) * (2 * (by_y & 1) - 1)
        x = my_x + x_step
        return ((x & 1) << 5) + ((y & 3) << 3) + (z & 7)

    line_mates = [(my_z + step) & 7 for step in (4, 5, 3, 6, 2, 7, 1)]
    plane_mates = [
        (((my_x + x_step) & 1) << 2) + ((my_y + y_step) & 3)
        for x_step, y_step in ((1, 2), (1, 1), (1, 3), (0, 2), (1, 0), (0, 1), (0, 3))
    ]

    def in_half(line, z):
        return device(group * HALF + line * 8 + z)

    barrier = pltpu.get_barrier_semaphore()

    def greet(target):
        pl.semaphore_signal(barrier, inc=1, device_id=target, device_id_type=MESH)

    for z in line_mates:
        greet(in_half(my_line, z))
    for line in plane_mates:
        greet(in_half(line, my_z))
    greet(other_core)

    @pl.when(group == 0)
    def _():
        greet(device(HALF + me))

    for load in loads:
        load.start()

    signs = sign_matrix()
    signs_twice = jnp.concatenate([signs, signs], axis=0)
    signs_ref[...] = signs_twice
    slot_ids = lax.broadcasted_iota(jnp.int32, (LANES, 64), 1)
    site_ids = lax.broadcasted_iota(jnp.int32, (LANES, 64), 0)
    forward = (row == 0).astype(F32)
    for load in loads:
        load.wait()
    keep, turn, source, decays, angles = [], [], [], [], []
    for p in range(2):
        hour = p + row * (1 - 2 * p)
        decay = forward * fwd_ref[pl.ds(hour, 1), :] + (1.0 - forward) * bwd_ref[pl.ds(hour, 1), :]
        angle = jnp.full((1, 2 * LANES), angle_ref[hour], F32)
        cosine = jnp.cos(angle)
        sine = jnp.sin(angle) * ((2.0 * forward - 1.0) / math.sqrt(LANES))
        kept = decay * cosine
        turned = decay * sine
        keep.append((kept[:, :LANES], kept[:, LANES:]))
        turn.append((-turned[:, :LANES], turned[:, LANES:]))
        decays.append((decay[:, :LANES], decay[:, LANES:]))
        angles += [cosine[:, :LANES], sine[:, :LANES]]
        table = (
            (site_ids == sites_ref[pl.ds(hour, 1), :]) & (slot_ids < count_ref[hour])
        ).astype(F32).astype(BF16)
        values = values_ref[hour]
        first = values.astype(BF16)
        rest = values - first.astype(F32)
        second = rest.astype(BF16)
        third = (rest - second.astype(F32)).astype(BF16)
        sums = dot(table, jnp.concatenate([first, second, third], axis=1))
        sums = sums[:, :LANES] + (sums[:, LANES : 2 * LANES] + sums[:, 2 * LANES :])
        sums = sums.T
        gain = gain_ref[pl.ds(hour, 1), :]
        source.append((sums * gain[:, :LANES], sums * gain[:, LANES:]))
        for h in range(2):
            source_ref[p, h] = source[p][h]

    for h in range(2):
        both = (
            keep[1][h] * source[0][h]
            + turn[1][h] * times_signs(source[0][1 - h], signs_twice)
            + source[1][h]
        )
        for s in range(2):
            for z in range(8):
                first_share = s * HALF + z * 8
                outbox[z, pl.ds(2 * h + s, 8, stride=4), :] = both[first_share : first_share + 8]
    quarter = lax.broadcasted_iota(jnp.int32, (1, LANES), 1) // 32
    packed = angles[0]
    for i in range(1, 4):
        packed = jnp.where(quarter == i, angles[i], packed)
    own_coefs[0:1, :] = packed
    for h in range(2):
        for p in range(2):
            own_coefs[pl.ds(1 + 2 * h + p, 1), :] = decays[p][h]

    pl.semaphore_wait(barrier, 15 + group)

    def slot(ref, k, part):
        return ref.at[pl.ds(k * TILE + part[0], part[1]), :]

    def to_peer(src, dst, peer, send, recv):
        return pltpu.make_async_remote_copy(
            src_ref=src,
            dst_ref=dst,
            send_sem=send,
            recv_sem=recv,
            device_id=peer,
            device_id_type=MESH,
        )

    five = pl.ds(0, COEFS[1])
    my_pair = my_y >> 1
    quarters = [(x, pair) for x in (1 - my_x, my_x) for pair in (1 - my_pair, my_pair)]

    def share_sources(part):
        x, pair = quarters[part]
        rows = pl.ds(16 * x + 8 * pair, 8)
        for z in line_mates:
            to_peer(
                outbox.at[z, rows, :],
                line_sources.at[my_z, rows, :],
                in_half(my_line, z),
                send_sem.at[5],
                line_sem.at[3 + part],
            ).start()

    share_sources(0)
    share_sources(1)
    for line in plane_mates:
        to_peer(
            own_coefs.at[five, :],
            plane_coefs.at[my_line, five, :],
            in_half(line, my_z),
            send_sem.at[0],
            line_sem.at[0],
        ).start()
    share_sources(2)
    share_sources(3)
    plane_coefs[my_line] = own_coefs[...]
    line_sources[my_z] = outbox[my_z]

    def bulk(ref, count, part, send, recv):
        rows = ref.at[pl.ds(0, count * part[1]), :]
        return to_peer(rows, rows, device(place), send, recv)

    def seven(ref, rows, send, recv):
        part = ref.at[pl.ds(0, 7), pl.ds(0, rows), :]
        return to_peer(part, part, device(place), send, recv)

    seven(plane_coefs, COEFS[1], send_sem.at[0], line_sem.at[0]).wait_recv()
    def pass_coefs(part):
        lines = pl.ds(4 * part, 4)
        for z in line_mates:
            to_peer(
                plane_coefs.at[lines, five, :],
                inbox.at[lines, my_z, pl.ds(*COEFS), :],
                in_half(my_line, z),
                send_sem.at[7],
                line_sem.at[1 + part],
            ).start()

    pass_coefs(0)
    for part, (x, pair) in enumerate(quarters):
        seven(line_sources, 8, send_sem.at[5], line_sem.at[3 + part]).wait_recv()
        for other in (1, 0)[: 2 - part // 3]:
            line = x * 4 + pair * 2 + (((my_y & 1) + other) & 1)
            to_peer(
                line_sources.at[:, pl.ds(line * 4, 4), :],
                inbox.at[my_line, :, pl.ds(*SOURCES), :],
                in_half(line, my_z),
                send_sem.at[6],
                inbox_sem.at[my_line],
            ).start()
    pass_coefs(1)
    for k in range(8):
        inbox[k, my_z, pl.ds(*COEFS), :] = plane_coefs[k, five, :]
        inbox[my_line, k, pl.ds(*SOURCES), :] = line_sources[k, pl.ds(my_line * 4, 4), :]

    def second_leg(part, send, recv):
        rows = inbox.at[pl.ds(0, 7), :, pl.ds(0, part[1]), :]
        return to_peer(rows, rows, device(place), send, recv)

    def coefs_arrived(part):
        rows = inbox.at[pl.ds(0, 4), pl.ds(0, 7), pl.ds(0, COEFS[1]), :]
        to_peer(rows, rows, device(place), send_sem.at[7], line_sem.at[1 + part]).wait_recv()

    coefs_arrived(0)

    def chunk_arrived(c):
        @pl.when(c != my_line)
        def _():
            rows = inbox.at[0, :, pl.ds(0, SOURCES[1]), :]
            to_peer(rows, rows, device(place), send_sem.at[6], inbox_sem.at[c]).wait_recv()

    tile_row = lax.broadcasted_iota(jnp.int32, (8, LANES), 0)
    tile_lane = lax.broadcasted_iota(jnp.int32, (8, LANES), 1)
    upper = ((tile_row == 2) & (tile_lane == share)) | (
        (tile_row == 3) & (tile_lane == share + HALF)
    )
    lower = ((tile_row == 4) & (tile_lane == share)) | (
        (tile_row == 5) & (tile_lane == share + HALF)
    )

    def coefficients(b):
        sources = inbox[b >> 3, b & 7, pl.ds(0, 8), :]
        rows = inbox[b >> 3, b & 7, pl.ds(8, 8), :]
        cosine, sine, next_cosine, next_sine = [
            jnp.broadcast_to(rows[0:1, 32 * i : 32 * i + 1], (1, LANES)) for i in range(4)
        ]
        decay = rows[1:2], rows[3:4]
        next_decay = rows[2:3], rows[4:5]
        return (
            [d * cosine for d in decay],
            [-decay[0] * sine, decay[1] * sine],
            [d * next_cosine for d in next_decay],
            [-next_decay[0] * next_sine, next_decay[1] * next_sine],
            sources,
        )

    def twice_turned(coefs):
        parts = []
        for turn_row in (coefs[1][1], coefs[1][0]):
            high, low = split(turn_row)
            left = jnp.concatenate(
                [signs_ref[:LANES, :] * high, signs_ref[:LANES, :] * low], axis=1
            )
            parts.append(split(dot(left, signs_ref[...])))
        (u_high, u_low), (l_high, l_low) = parts
        return jnp.concatenate(
            [
                jnp.concatenate([u_high, l_high], axis=1),
                jnp.concatenate([u_low, l_low], axis=1),
            ],
            axis=0,
        )

    def block(x, coefs, weights):
        keep_rows, turn_rows, next_keep, next_turn, sources = coefs
        high, low = split(x)
        kept = jnp.concatenate([keep_rows[0] * x[:8], keep_rows[1] * x[8:]], axis=0)
        turned = dot(
            jnp.concatenate(
                [
                    jnp.concatenate([high, low], axis=1),
                    jnp.concatenate(split(kept), axis=1),
                ],
                axis=0,
            ),
            signs_ref[...],
        )
        both = dot(
            jnp.concatenate(
                [
                    jnp.concatenate([high, high], axis=1),
                    jnp.concatenate([low, jnp.zeros_like(low)], axis=1),
                ],
                axis=0,
            ),
            weights,
        )
        source_u = jnp.where(tile_row >= 6, pltpu.roll(sources, 2, 0), 0.0)
        source_l = jnp.where(tile_row >= 6, sources, 0.0)
        u = (
            (next_keep[0] * kept[:8] + source_u)
            + (next_keep[0] * turn_rows[0]) * turned[8:16]
            + next_turn[0] * (turned[24:] + (both[:8, :LANES] + both[16:24, :LANES]))
        )
        l = (
            (next_keep[1] * kept[8:] + source_l)
            + (next_keep[1] * turn_rows[1]) * turned[:8]
            + next_turn[1] * (turned[16:24] + (both[8:16, LANES:] + both[24:, LANES:]))
        )
        return jnp.concatenate([u, l], axis=0)

    def keep_state(ref, at, x):
        ref[pl.ds(pl.multiple_of(at, TILE), 8), :] = x[:8]
        ref[pl.ds(at + 8, 2), :] = x[14:]
        ref[pl.ds(at + 10, 4), :] = x[10:14]

    def run(part):
        def run_chunk(c, carried):
            x, weights = carried

            for i in range(STEPS // 8):
                chunk_arrived(c * (STEPS // 8) + i)

            @pl.when(c == HALF // STEPS // 2 - 1)
            def _():
                coefs_arrived(1)

            if part is STATE:
                @pl.when(c == HALF // STEPS - 1)
                def _():
                    pl.semaphore_signal(
                        ready_sem, inc=1, device_id=device(me), device_id_type=MESH
                    )

            def send(b):
                own = (b == me).astype(jnp.int32)
                peer = b + own * (me + 1 - 2 * (me & 1) - b)
                to_peer(
                    slot(history, b, part),
                    slot(before, share + own * (HALF - share), part),
                    device(group * HALF + peer),
                    send_sem.at[1],
                    recv_sem.at[1],
                ).start()

            for k in range(STEPS):
                b = c * STEPS + k
                keep_state(history, b * TILE, x)
                following = twice_turned(coefficients(jnp.minimum(b + 1, HALF - 1)))
                x = block(x, coefficients(b), weights)
                weights = following
                if k % 2 == 1:
                    send(b - 1)
                    send(b)
            return x, weights

        x = jnp.concatenate([upper.astype(F32), lower.astype(F32)], axis=0)
        x, _ = lax.fori_loop(0, HALF // STEPS, run_chunk, (x, twice_turned(coefficients(0))))
        keep_state(final, 0, x)

    @pl.when(group == 0)
    def _():
        run(SAMPLES)
        pl.semaphore_wait(ready_sem, 1)

        def conclude(k, carry):
            peer = ranked(k, k & 1)
            to_peer(
                slot(final, 0, SAMPLES),
                slot(ends, share, SAMPLES),
                device(HALF + peer),
                send_sem.at[2],
                recv_sem.at[2],
            ).start()
            return carry

        lax.fori_loop(0, HALF, conclude, 0)
        bulk(before, HALF, SAMPLES, send_sem.at[1], recv_sem.at[1]).wait_recv()

    @pl.when(group == 1)
    def _():
        run(STATE)
        bulk(before, HALF, STATE, send_sem.at[1], recv_sem.at[1]).wait_recv()

    before[pl.ds(pl.multiple_of(share * TILE, TILE), TILE), :] = history[
        pl.ds(pl.multiple_of(me * TILE, TILE), TILE), :
    ]

    def gathered(ref, at):
        return ref[pl.ds(at, HALF, stride=TILE), :]

    def hour_of(p):
        return p + row * (1 - 2 * p)

    def swap(p):
        hour = hour_of(p)
        return to_peer(
            mine_ref.at[1, hour],
            theirs_ref.at[hour],
            other_core,
            send_sem.at[3 + p],
            recv_sem.at[3 + hour],
        )

    def own_hours(with_transfer):
        halves = [
            jnp.concatenate([gathered(before, 6 + 2 * h + s) for s in range(2)], axis=0)
            for h in range(2)
        ]
        if with_transfer:
            halves = [
                jnp.concatenate(
                    [halves[h]] + [gathered(before, 2 + 8 * h + i) for i in range(4)], axis=0
                )
                for h in range(2)
            ]
        count = halves[0].shape[0]
        for p in range(2):
            turned = times_signs(jnp.concatenate(halves, axis=0), signs_ref[...])
            halves = [
                keep[p][0] * halves[0] + turn[p][0] * turned[count:],
                keep[p][1] * halves[1] + turn[p][1] * turned[:count],
            ]
            bare = [half[:LANES] for half in halves]
            full = [bare[h] + source_ref[p, h] for h in range(2)]
            mine_ref[0, hour_of(p)] = jnp.where(row == 0, full[0], bare[1])
            mine_ref[1, hour_of(p)] = jnp.where(row == 0, full[1], bare[0])
            if with_transfer:
                columns = [half[LANES:] for half in halves]
                for q in range(2):
                    chosen = jnp.where(row == 0, columns[q], columns[1 - q])
                    moves_ref[p, q, 0], moves_ref[p, q, 1] = split(chosen)
                full = [jnp.concatenate([full[h], columns[h]], axis=0) for h in range(2)]
            else:
                swap(p).start()
            halves = full

    @pl.when(group == 0)
    def _():
        own_hours(False)

    @pl.when(group == 1)
    def _():
        own_hours(True)
        bulk(ends, HALF, SAMPLES, send_sem.at[2], recv_sem.at[2]).wait_recv()
        entry = jnp.concatenate(
            [
                jnp.concatenate([gathered(ends, 6 + 2 * h + s) for h in range(2)], axis=1)
                for s in range(2)
            ],
            axis=0,
        )
        entry_high, entry_low = split(entry)
        entry_both = jnp.concatenate([entry_high, entry_low], axis=0)
        for q in (1, 0):
            for p in range(2):
                moved = dot(entry_both, moves_ref[p, q, 0])
                mine_ref[q, hour_of(p)] += moved[:LANES] + (
                    moved[LANES:] + dot(entry_high, moves_ref[p, q, 1])
                )
                if q == 1:
                    swap(p).start()

    for hour in range(2):
        pltpu.make_async_remote_copy(
            src_ref=theirs_ref.at[hour],
            dst_ref=theirs_ref.at[hour],
            send_sem=send_sem.at[3],
            recv_sem=recv_sem.at[3 + hour],
            device_id=other_core,
            device_id_type=MESH,
        ).wait_recv()
        own = mine_ref[0, hour]
        their = theirs_ref[hour]
        own_ref[hour] = own.T
        their_ref[hour] = their.T

    seven(plane_coefs, COEFS[1], send_sem.at[0], line_sem.at[0]).wait_send()
    seven(line_sources, 32, send_sem.at[5], line_sem.at[1]).wait_send()
    second_leg(SOURCES, send_sem.at[6], line_sem.at[0]).wait_send()
    second_leg(COEFS, send_sem.at[7], line_sem.at[0]).wait_send()

    @pl.when(group == 0)
    def _():
        bulk(history, HALF, SAMPLES, send_sem.at[1], recv_sem.at[1]).wait_send()
        bulk(ends, HALF, SAMPLES, send_sem.at[2], recv_sem.at[2]).wait_send()

    @pl.when(group == 1)
    def _():
        bulk(history, HALF, STATE, send_sem.at[1], recv_sem.at[1]).wait_send()

    for p in range(2):
        swap(p).wait_send()


def local(decay_fwd, decay_bwd, angle, gain, obs_values, obs_sites, obs_count):
    args = (decay_fwd, decay_bwd, angle, gain, obs_values, obs_sites, obs_count)
    vmem = pl.BlockSpec(memory_space=pltpu.VMEM)
    out = jax.ShapeDtypeStruct((2, LANES, LANES), F32)
    box = pltpu.VMEM((HALF * TILE, LANES), F32)
    own, their = pl.pallas_call(
        kernel,
        out_shape=(out, out),
        in_specs=[pl.BlockSpec(memory_space=pl.ANY)] * len(args),
        out_specs=(vmem, vmem),
        scratch_shapes=[
            *(
                (pltpu.SMEM if arg.ndim == 1 else pltpu.VMEM)(arg.shape, arg.dtype)
                for arg in args
            ),
            pltpu.VMEM((8, 32, LANES), F32),
            pltpu.VMEM((8, LANES), F32),
            pltpu.VMEM((8, 32, LANES), F32),
            pltpu.VMEM((8, 8, LANES), F32),
            pltpu.VMEM((8, 8, TILE, LANES), F32),
            box,
            pltpu.VMEM(((HALF + 1) * TILE, LANES), F32),
            pltpu.VMEM((TILE, LANES), F32),
            box,
            pltpu.VMEM((2 * LANES, LANES), BF16),
            pltpu.VMEM((2, 2, LANES, LANES), F32),
            pltpu.VMEM((2, 2, 2, 2 * LANES, LANES), BF16),
            pltpu.VMEM((2, 2, LANES, LANES), F32),
            pltpu.VMEM((2, LANES, LANES), F32),
            pltpu.SemaphoreType.DMA((len(args),)),
            pltpu.SemaphoreType.DMA((8,)),
            pltpu.SemaphoreType.DMA((5,)),
            pltpu.SemaphoreType.DMA((7,)),
            pltpu.SemaphoreType.DMA((8,)),
            pltpu.SemaphoreType.REGULAR,
        ],
        compiler_params=pltpu.CompilerParams(
            collective_id=1, has_side_effects=True, vmem_limit_bytes=32 * 2**20
        ),
        name="smoother",
    )(*(pltpu.with_memory_space_constraint(arg, pltpu.HBM) for arg in args))
    return jnp.where(lax.axis_index("row") == 0, own, their), own + their


def solution(mesh):
    return jax.shard_map(
        local,
        mesh=mesh,
        in_specs=(
            P("tm", None),
            P("tm", None),
            P("tm"),
            P("tm", None),
            P("tm", None, None),
            P("tm", None),
            P("tm"),
        ),
        out_specs=(P("tm", "row", None), P("tm", "row", None)),
        check_vma=False,
    )
```
